128 devices in a mesh: tm: 32 (over y, x, z_hi), row: 2 (over z_lo), col: 2 (over core).
Axes of the slice: x: 4, y: 4, z: 4 (z_hi: 2, z_lo: 2; z = z_hi * 2 + z_lo), core: 2. Of those that a mesh axis runs over, the one named last changes fastest.
Arguments:
- strain: float32 [24576, 2048], P('tm', ('row', 'col')), may hold values from -6 to 6
Outputs:
- lag_corr: float32 [2048, 8, 2048], P(('tm', 'row'), None, 'col')
The draws below stay inside these ranges and needn't reach their ends.
All inputs are finite; a program needn't handle non-finite values.
Results may differ from the reference program's by a relative error of at most 0.0001.
Values sent between devices are 32-bit elements; how exact they have to be, the bound alone decides.
A program may use at most 192 MiB of HBM per device.

```python
import jax
import jax.numpy as jnp
from jax import lax

C = 2048
LAGS = 8
SAMPLES = 24576


def block_scale(rng, shape, cuts, low, high):
    level, own = 1.0, jax.random.fold_in(rng, 6)
    for dim, blocks in cuts:
        steps = jnp.exp(jax.random.uniform(jax.random.fold_in(own, dim), (blocks,), jnp.float32, low / len(cuts), high / len(cuts)))
        level = level * jnp.repeat(steps, shape[dim] // blocks).reshape([-1 if axis == dim else 1 for axis in range(len(shape))])
    return level


def scatter_about(stream_key, extent, spread, bound, split=(), held_as=jnp.bfloat16):
    result = jax.random.normal(stream_key, extent, jnp.float32) * spread
    if len(split) > 0:
        result = block_scale(stream_key, extent, split, -0.22, 0.18) * result
    return jnp.clip(result, min=-bound, max=bound).astype(held_as)


def setup_inputs(seed: int = 0) -> dict:
    splits = jax.random.split(jax.random.key(seed), 2)
    strain = scatter_about(splits[0], (SAMPLES, C), 1.0, 6.0, ((0, 32), (1, 4)), jnp.float32)
    return {"strain": strain}


def reference(strain):
    total = strain.shape[0]
    blocks = []
    for lag in range(1, LAGS + 1):
        ahead = strain[lag:]
        behind = strain[:total - lag]
        prod = jnp.dot(ahead.T, behind, precision=lax.Precision.HIGHEST, preferred_element_type=jnp.float32)
        blocks.append(prod / jnp.sqrt(jnp.float32(total - lag)))
    return jnp.stack(blocks, axis=1)
```

```python
import functools

import jax
import jax.numpy as jnp
import numpy as np
from jax import lax
from jax.experimental import pallas as pl
from jax.experimental.pallas import tpu as pltpu
from jax.sharding import PartitionSpec as P

MESH = pl.DeviceIdType.MESH
LAGS = 8
SAMPLES = 24576
LEN = 768
LANES = 128
PER = LEN // LAGS
DEEP = 4 * PER
WIDE = 2 * LANES
F32 = jnp.float32
BF16 = jnp.bfloat16


def halves(v):
    hi = v.astype(BF16)
    return hi, (v - hi.astype(F32)).astype(BF16)


def kernel(
    s_ref, out_ref, blocks, firsts, halo, halo_out, x_hi, x_lo, y_hi, y_lo, part, far_in, near_in, last_in,
    load_sem, copy_sem, halo_sem, fan_send, fan_recv, fan_copy, ring_send, ring_recv, z_send, z_recv,
    core_send, core_recv, far_send, far_recv, near_send, near_recv, last_send, last_recv, last_copy,
):
    tm, zl, c = lax.axis_index("tm"), lax.axis_index("row"), lax.axis_index("col")
    y, x, zh = lax.div(tm, 8), lax.rem(lax.div(tm, 2), 4), lax.rem(tm, 2)
    b = zl * 2 + c

    def at(yy, xx, zz, row, col):
        return (lax.rem(yy, 4) * 8 + lax.rem(xx, 4) * 2 + zz, row, col)

    def along_x(d):
        return at(y, x + d, zh, zl, c)

    def along_y(d):
        return at(y + d, x, zh, zl, c)

    before = (lax.rem(tm + 31, 32), zl, c)
    after = (lax.rem(tm + 1, 32), zl, c)
    other_z = (tm, 1 - zl, c)
    other_core = (tm, zl, 1 - c)

    barrier = pltpu.get_barrier_semaphore()
    peers = [along_x(1), along_x(2), along_x(3), along_y(1), along_y(3), before, after]
    peers += [(tm, 1 - zl, c), (tm, 1 - zl, 1 - c), (tm, zl, 1 - c)]
    peers += [at(y, x, 1 - zh, row, col) for row in (0, 1) for col in (0, 1)]
    for peer in peers:
        pl.semaphore_signal(barrier, inc=1, device_id=peer, device_id_type=MESH)

    loads = []
    for q in range(4):
        lanes = pl.ds(pl.multiple_of(lax.rem(x + q, 4) * LANES, LANES), LANES)
        loads.append(pltpu.make_async_copy(s_ref.at[:, lanes], blocks.at[0, q], load_sem.at[q]))
        loads[-1].start()
    pl.semaphore_wait(barrier, len(peers))

    sent = []

    def send(src, dst, send_sem, recv_sem, device):
        copy = pltpu.make_async_remote_copy(
            src_ref=src, dst_ref=dst, send_sem=send_sem, recv_sem=recv_sem, device_id=device, device_id_type=MESH
        )
        copy.start()
        sent.append(copy)
        return copy

    def ring(way, n, d, q):
        step = 3 if way == 0 else 1
        return send(
            blocks.at[d, q],
            blocks.at[(d + step) % 4, (q + step) % 4],
            ring_send.at[way, n],
            ring_recv.at[way, n],
            along_x(1 if way == 0 else 3),
        )

    halo_copy = send(s_ref.at[pl.ds(0, LAGS)], halo, halo_sem.at[0], halo_sem.at[1], before)
    for load in loads:
        load.wait()

    r0, l0 = ring(0, 0, 0, 1), ring(1, 0, 0, 3)
    r1, l1 = ring(0, 1, 0, 2), ring(1, 1, 0, 0)

    halo_copy.wait_recv()
    for p in range(4):
        halo_out[p] = jnp.where(tm == 31, jnp.zeros((LAGS, LANES), F32), halo[:, p * LANES : (p + 1) * LANES])
    tail = pl.ds(LEN, LAGS)
    fans = []
    for d in range(1, 4):
        fans.append(
            send(
                halo_out.at[lax.rem(x + d, 4)],
                firsts.at[b, 4 - d, tail],
                fan_send.at[4 - d],
                fan_recv.at[4 - d],
                along_x(d),
            )
        )
    fan0 = pltpu.make_async_copy(halo_out.at[x], firsts.at[b, 0, tail], fan_copy.at[0])
    fan0.start()

    z_copies, core_copies = {}, {}

    def cross(d, arrived):
        if arrived is not None:
            arrived.wait_recv()
        mine = pltpu.make_async_copy(blocks.at[d, 0], firsts.at[b, d, pl.ds(0, LEN)], copy_sem.at[d])
        mine.start()
        if d == 0:
            fan0.wait()
        else:
            fans[3 - d].wait_recv()
        mine.wait()
        z_copies[d] = send(firsts.at[b, d], firsts.at[b, d], z_send.at[d], z_recv.at[d], other_z)
        core_copies[d] = send(firsts.at[b, d], firsts.at[b, d], core_send.at[0, d], core_recv.at[0, d], other_core)

    def pass_on(d):
        z_copies[d].wait_recv()
        b2 = (1 - zl) * 2 + c
        core_copies[4 + d] = send(
            firsts.at[b2, d], firsts.at[b2, d], core_send.at[1, d], core_recv.at[1, d], other_core
        )

    cross(0, None)
    cross(3, r0)
    cross(1, l0)
    r1.wait_recv()
    r2 = ring(0, 2, 3, 1)
    l2 = ring(1, 2, 1, 0)
    cross(2, r2)
    r3, l3 = ring(0, 3, 0, 3), ring(1, 3, 0, 1)
    r4 = ring(0, 4, 0, 0)
    l1.wait_recv()
    l4 = ring(1, 4, 1, 1)
    r5, l5 = ring(0, 5, 3, 0), ring(1, 5, 0, 2)
    for d in (0, 3, 1, 2):
        pass_on(d)
    l2.wait_recv()

    def seconds(chunk):
        for q in range(2):
            lanes = slice(q * LANES, (q + 1) * LANES)
            for d in range(4):
                for r in range(LAGS):
                    hi, lo = halves(blocks[d, 2 * chunk + q, pl.ds(r, PER, stride=LAGS), :])
                    rows = slice(r * DEEP + d * PER, r * DEEP + (d + 1) * PER)
                    y_hi[rows, lanes] = hi
                    y_lo[rows, lanes] = lo

    def spread(bb, carry):
        for m in range(1, 2 * LAGS):
            v = jnp.concatenate([firsts[bb, d, pl.ds(m, PER, stride=LAGS), :] for d in range(4)], axis=0)
            hi, lo = halves(v.T)
            lanes = slice((m - 1) * DEEP, m * DEEP)
            x_hi[bb, :, lanes] = hi
            x_lo[bb, :, lanes] = lo
        return carry

    def products(chunk, e):
        bb = lax.rem(y + e, 4)

        def dots(n):
            lhs_hi = jnp.concatenate(
                [x_hi[bb, :, pl.ds(pl.multiple_of(n * LEN + k * DEEP, LANES), LEN)] for k in range(LAGS)], axis=0
            )
            lhs_lo = jnp.concatenate(
                [x_lo[bb, :, pl.ds(pl.multiple_of(n * LEN + k * DEEP, LANES), LEN)] for k in range(LAGS)], axis=0
            )
            rows = pl.ds(pl.multiple_of(n * LEN, LEN), LEN)
            rhs_hi, rhs_lo = y_hi[rows, :], y_lo[rows, :]
            got = jnp.dot(lhs_hi, rhs_hi, preferred_element_type=F32)
            got += jnp.dot(lhs_lo, rhs_hi, preferred_element_type=F32)
            got += jnp.dot(lhs_hi, rhs_lo, preferred_element_type=F32)
            return got.reshape(LAGS, LANES, WIDE)

        def step(n, carry):
            part[chunk, e] += dots(n)
            return carry

        part[chunk, e] = dots(0)
        lax.fori_loop(1, 4, step, 0)

    half = [pl.ds(0, LAGS // 2), pl.ds(LAGS // 2, LAGS // 2)]
    fars, nears, lasts = {}, {}, {}

    def near(chunk, way, h):
        e = 1 if way == 0 else 3
        nears[chunk, way, h] = send(
            part.at[chunk, e, half[h]],
            near_in.at[chunk, way, half[h]],
            near_send.at[chunk, way, h],
            near_recv.at[chunk, way, h],
            along_y(e),
        )

    def sums(chunk):
        products(chunk, 2)
        for way in range(2):
            fars[chunk, way] = send(
                part.at[chunk, 2, half[way]],
                far_in.at[chunk, way],
                far_send.at[chunk, way],
                far_recv.at[chunk, way],
                along_y(1 if way == 0 else 3),
            )
        products(chunk, 1)
        near(chunk, 0, 1)
        products(chunk, 3)
        near(chunk, 1, 0)
        products(chunk, 0)

    def add_far(chunk):
        for way in range(2):
            e = 1 if way == 0 else 3
            fars[chunk, way].wait_recv()
            part[chunk, e, half[way]] += far_in[chunk, way]
            near(chunk, way, way)

    def finish(chunk):
        for way in range(2):
            for h in range(2):
                nears[chunk, way, h].wait_recv()
        part[chunk, 0] += near_in[chunk, 0] + near_in[chunk, 1]
        for other in range(2):
            for row in range(2):
                src = part.at[chunk, 0, :, pl.ds(pl.multiple_of((lax.rem(zh + other, 2) * 2 + row) * 32, 32), 32)]
                here = jnp.logical_and(row == zl, zl == c) if other == 0 else False
                copy = pltpu.make_async_remote_copy(
                    src_ref=src,
                    dst_ref=last_in.at[chunk, c, zh],
                    send_sem=last_send.at[chunk, other, row],
                    recv_sem=last_recv.at[chunk, c, zh],
                    device_id=at(y, x, lax.rem(zh + other, 2), row, zl),
                    device_id_type=MESH,
                )
                if other == 0:
                    pl.when(jnp.logical_not(here))(copy.start)
                    own = pltpu.make_async_copy(src, last_in.at[chunk, c, zh], last_copy.at[chunk])
                    lasts[chunk, row] = (here, copy, own)
                    pl.when(here)(own.start)
                else:
                    copy.start()
                    sent.append(copy)

    scale = [np.float32(1.0 / np.sqrt(np.float32(SAMPLES - k))) for k in range(1, LAGS + 1)]

    def write(chunk):
        for row in range(2):
            here, copy, own = lasts[chunk, row]
            pl.when(jnp.logical_not(here))(copy.wait_send)
            pl.when(here)(own.wait)
        for cc in range(2):
            for hh in range(2):
                arrives = jnp.logical_not(jnp.logical_and(zl == c, jnp.logical_and(cc == c, hh == zh)))
                copy = pltpu.make_async_remote_copy(
                    src_ref=last_in.at[chunk, cc, hh],
                    dst_ref=last_in.at[chunk, cc, hh],
                    send_sem=last_send.at[chunk, 0, 0],
                    recv_sem=last_recv.at[chunk, cc, hh],
                    device_id=other_z,
                    device_id_type=MESH,
                )
                pl.when(arrives)(copy.wait_recv)
        for cc in range(2):
            for q in range(2):
                p = lax.rem(x + 2 * chunk + q, 4)
                lanes = pl.ds(pl.multiple_of(cc * 4 * LANES + p * LANES, LANES), LANES)
                for k in range(LAGS):
                    piece = slice(q * LANES, (q + 1) * LANES)
                    total = last_in[chunk, cc, 0, k, :, piece] + last_in[chunk, cc, 1, k, :, piece]
                    out_ref[:, k, lanes] = total * scale[k]

    seconds(0)
    for d in range(4):
        core_copies[d].wait_recv()
        core_copies[4 + d].wait_recv()
    lax.fori_loop(0, 4, spread, 0)
    sums(0)
    add_far(0)
    for copy in (r3, l3, r4, l4, r5, l5):
        copy.wait_recv()
    seconds(1)
    sums(1)
    finish(0)
    add_far(1)
    finish(1)
    write(0)
    write(1)
    for copy in sent:
        copy.wait_send()


def shards(strain):
    dma = pltpu.SemaphoreType.DMA
    return pl.pallas_call(
        kernel,
        out_shape=jax.ShapeDtypeStruct((32, LAGS, 8 * LANES), F32),
        in_specs=[pl.BlockSpec(memory_space=pl.ANY)],
        out_specs=pl.BlockSpec(memory_space=pltpu.VMEM),
        scratch_shapes=[
            pltpu.VMEM((4, 4, LEN, LANES), F32),
            pltpu.VMEM((4, 4, LEN + LAGS, LANES), F32),
            pltpu.VMEM((LAGS, 4 * LANES), F32),
            pltpu.VMEM((4, LAGS, LANES), F32),
            pltpu.VMEM((4, LANES, (2 * LAGS - 1) * DEEP), BF16),
            pltpu.VMEM((4, LANES, (2 * LAGS - 1) * DEEP), BF16),
            pltpu.VMEM((LAGS * DEEP, WIDE), BF16),
            pltpu.VMEM((LAGS * DEEP, WIDE), BF16),
            pltpu.VMEM((2, 4, LAGS, LANES, WIDE), F32),
            pltpu.VMEM((2, 2, LAGS // 2, LANES, WIDE), F32),
            pltpu.VMEM((2, 2, LAGS, LANES, WIDE), F32),
            pltpu.VMEM((2, 2, 2, LAGS, 32, WIDE), F32),
            dma((4,)), dma((4,)), dma((2,)), dma((4,)), dma((4,)), dma((1,)), dma((2, 6)), dma((2, 6)),
            dma((4,)), dma((4,)), dma((2, 4)), dma((2, 4)), dma((2, 2)), dma((2, 2)),
            dma((2, 2, 2)), dma((2, 2, 2)), dma((2, 2, 2)), dma((2, 2, 2)), dma((2,)),
        ],
        compiler_params=pltpu.CompilerParams(
            collective_id=0, has_side_effects=True, vmem_limit_bytes=60 * 2**20
        ),
        cost_estimate=pl.CostEstimate(flops=3 * 2 * 8 * 512 * 512 * 3072, bytes_accessed=2**22, transcendentals=0),
    )(strain)


def solution(mesh):
    placed = (P("tm", ("row", "col")),)
    return jax.shard_map(
        shards, mesh=mesh, in_specs=placed, out_specs=P(("tm", "row"), None, "col"), check_vma=False
    )
```

```python
import jax
import jax.numpy as jnp
import numpy as np
from jax import lax
from jax.experimental import pallas as pl
from jax.experimental.pallas import tpu as pltpu
from jax.sharding import PartitionSpec as P

MESH = pl.DeviceIdType.MESH
LAGS = 8
SAMPLES = 24576
LEN = 768
LANES = 128
PER = LEN // LAGS
DEEP = 4 * PER
CHUNKS = ((0, 2), (2, 2))
WIDTHS = tuple(n * LANES for _, n in CHUNKS)
F32 = jnp.float32
BF16 = jnp.bfloat16


def halves(v):
    hi = v.astype(BF16)
    return hi, (v - hi.astype(F32)).astype(BF16)


def kernel(
    s_ref, out_ref, blocks, firsts, heads, heads_z, head_y, tails, x_hi, x_lo, y_hi, y_lo, part, far_in, near_in, last_in,
    load_sem, own_sem, fan_send, fan_recv, fan_own, head_send, head_recv, ring_send, ring_recv, z_send, z_recv,
    core_send, core_recv, far_send, far_recv, near_send, near_recv, last_send, last_recv, last_own, ready,
):
    tm, zl, c = lax.axis_index("tm"), lax.axis_index("row"), lax.axis_index("col")
    y, x, zh = lax.div(tm, 8), lax.rem(lax.div(tm, 2), 4), lax.rem(tm, 2)
    b = zl * 2 + c
    b_z, b_core, b_both = (1 - zl) * 2 + c, zl * 2 + 1 - c, (1 - zl) * 2 + 1 - c

    def at(yy, xx, zz, row, col):
        return (lax.rem(yy, 4) * 8 + lax.rem(xx, 4) * 2 + zz, row, col)

    def along_x(d):
        return at(y, x + d, zh, zl, c)

    def along_y(d):
        return at(y + d, x, zh, zl, c)

    other_z = (tm, 1 - zl, c)
    other_core = (tm, zl, 1 - c)
    other_half = at(y, x, 1 - zh, zl, c)

    barrier = pltpu.get_barrier_semaphore()
    peers = [along_x(1), along_x(3), along_x(2), along_y(1), along_y(3), other_z, other_core, other_half]
    for peer in peers:
        pl.semaphore_signal(barrier, inc=1, device_id=peer, device_id_type=MESH)

    loads = []
    for q in (1, 3, 2, 0):
        lanes = pl.ds(pl.multiple_of(lax.rem(x + q, 4) * LANES, LANES), LANES)
        loads.append(pltpu.make_async_copy(s_ref.at[:, lanes], blocks.at[0, q], load_sem.at[q]))
        loads[-1].start()
    for load in loads:
        load.wait()
    pl.semaphore_wait(barrier, len(peers))

    sent = []

    def send(src, dst, send_sem, recv_sem, device):
        copy = pltpu.make_async_remote_copy(
            src_ref=src, dst_ref=dst, send_sem=send_sem, recv_sem=recv_sem, device_id=device, device_id_type=MESH
        )
        copy.start()
        sent.append(copy)
        return copy

    def ring(n, way, d, q):
        return send(
            blocks.at[d, q],
            blocks.at[(d - way) % 4, (q - way) % 4],
            ring_send.at[n],
            ring_recv.at[n],
            along_x(way % 4),
        )

    fans = []
    for d in range(1, 4):
        fans.append(
            send(blocks.at[0, d, pl.ds(0, LAGS)], heads.at[x], fan_send.at[4 - d], fan_recv.at[4 - d], along_x(d))
        )
    fan_mine = pltpu.make_async_copy(blocks.at[0, 0, pl.ds(0, LAGS)], heads.at[x], fan_own.at[0])
    fan_mine.start()

    from_left = ring(0, 1, 0, 1)
    from_right = ring(1, -1, 0, 3)

    z_copies, core_copies, own_copies = {}, {}, {}
    rows = pl.ds(0, LEN)
    tail = pl.ds(LEN, LAGS)
    farthest = lax.rem(y + 2, 4)

    def cross(d):
        z_copies[d] = pltpu.make_async_remote_copy(
            src_ref=blocks.at[d, 0],
            dst_ref=firsts.at[b, d, rows],
            send_sem=z_send.at[d],
            recv_sem=z_recv.at[d],
            device_id=other_z,
            device_id_type=MESH,
        )
        sent.append(z_copies[d])
        if d == 2:
            pl.when(b_core != farthest)(z_copies[d].start)
        else:
            z_copies[d].start()
        core_copies[d] = send(
            blocks.at[d, 0], firsts.at[b, d, rows], core_send.at[0, d], core_recv.at[0, d], other_core
        )
        own_copies[d] = pltpu.make_async_copy(blocks.at[d, 0], firsts.at[b, d, rows], own_sem.at[d])
        own_copies[d].start()

    def pass_on(d):
        z_copies[d].wait_recv()
        core_copies[5 + d].start()

    for d in range(5):
        src = firsts.at[b_z, :, tail] if d == 4 else firsts.at[b_z, d, rows]
        core_copies[5 + d] = pltpu.make_async_remote_copy(
            src_ref=src,
            dst_ref=src,
            send_sem=core_send.at[1, d],
            recv_sem=core_recv.at[1, d],
            device_id=other_core,
            device_id_type=MESH,
        )
        sent.append(core_copies[5 + d])

    fan_mine.wait()
    for copy in fans:
        copy.wait_recv()
    over_z = send(heads, heads_z, head_send.at[0], head_recv.at[0], other_half)
    cross(0)

    from_left.wait_recv()
    left_1, right_1 = ring(2, 1, 0, 2), ring(3, -1, 0, 0)
    cross(3)
    from_right.wait_recv()
    cross(1)
    over_z.wait_recv()
    over_y = send(heads_z.at[0], head_y, head_send.at[1], head_recv.at[1], along_y(3))
    left_1.wait_recv()
    from_far, far_1 = ring(4, 1, 3, 1), ring(5, -1, 1, 0)
    over_y.wait_recv()
    for d in range(4):
        place = lax.rem(x + d, 4)
        beyond = jnp.where(y == 3, jnp.zeros((LAGS, LANES), F32), head_y[...])
        after = jnp.where(place == 3, beyond, heads_z[lax.rem(place + 1, 4)])
        tails[d] = jnp.where(zh == 0, heads_z[place], after)
    z_copies[4] = send(tails, firsts.at[b, :, tail], z_send.at[4], z_recv.at[4], other_z)
    core_copies[4] = send(tails, firsts.at[b, :, tail], core_send.at[0, 4], core_recv.at[0, 4], other_core)
    own_copies[4] = pltpu.make_async_copy(tails, firsts.at[b, :, tail], own_sem.at[4])
    own_copies[4].start()
    pass_on(0)
    right_1.wait_recv()
    from_far.wait_recv()
    cross(2)
    rest = [ring(6, 1, 0, 3), ring(7, -1, 0, 1), ring(8, -1, 1, 1), ring(9, 1, 0, 0), ring(10, -1, 0, 2), ring(11, 1, 3, 0)]
    far_1.wait_recv()
    for d in (3, 1, 4):
        pass_on(d)

    def seconds(chunk):
        first, count = CHUNKS[chunk]
        for q in range(count):
            lanes = slice(q * LANES, (q + 1) * LANES)
            for d in range(4):
                for r in range(LAGS):
                    hi, lo = halves(blocks[d, first + q, pl.ds(r, PER, stride=LAGS), :])
                    to = slice(r * DEEP + d * PER, r * DEEP + (d + 1) * PER)
                    y_hi[to, lanes] = hi
                    y_lo[to, lanes] = lo

    def arrived(bb):
        @pl.when(bb == b)
        def _():
            for d in range(5):
                own_copies[d].wait()

        @pl.when(bb == b_core)
        def _():
            for d in range(5):
                core_copies[d].wait_recv()

        @pl.when(bb == b_both)
        def _():
            for d in range(5):
                core_copies[5 + d].wait_recv()

    def spread(bb):
        for m in range(1, 2 * LAGS):
            v = jnp.concatenate([firsts[bb, d, pl.ds(m, PER, stride=LAGS), :] for d in range(4)], axis=0)
            hi, lo = halves(v.T)
            lanes = slice((m - 1) * DEEP, m * DEEP)
            x_hi[bb, :, lanes] = hi
            x_lo[bb, :, lanes] = lo

    def products(chunk, e):
        bb = lax.rem(y + e, 4)
        width = WIDTHS[chunk]

        def dots(n):
            lhs_hi = jnp.concatenate(
                [x_hi[bb, :, pl.ds(pl.multiple_of(n * LEN + k * DEEP, LANES), LEN)] for k in range(LAGS)], axis=0
            )
            lhs_lo = jnp.concatenate(
                [x_lo[bb, :, pl.ds(pl.multiple_of(n * LEN + k * DEEP, LANES), LEN)] for k in range(LAGS)], axis=0
            )
            deep = pl.ds(pl.multiple_of(n * LEN, LEN), LEN)
            rhs_hi, rhs_lo = y_hi[deep, :width], y_lo[deep, :width]
            got = jnp.dot(lhs_hi, rhs_hi, preferred_element_type=F32)
            got += jnp.dot(lhs_lo, rhs_hi, preferred_element_type=F32)
            got += jnp.dot(lhs_hi, rhs_lo, preferred_element_type=F32)
            return got.reshape(2, 2, 2, LANES, width)

        def step(n, carry):
            part[chunk][e] += dots(n)
            return carry

        part[chunk][e] = dots(0)
        lax.fori_loop(1, 4, step, 0)

    fars, nears, lasts = {}, {}, {}
    ends = (1, 3)

    def near(chunk, way, u, w):
        nears[chunk, way, u, w] = send(
            part[chunk].at[ends[way], u, w],
            near_in[chunk].at[way, u, w],
            near_send.at[chunk, way, u, w],
            near_recv.at[chunk, way, u, w],
            along_y(ends[way]),
        )

    def make(chunk, e):
        if chunk == 0:
            bb = lax.rem(y + e, 4)
            if e == 2:
                pl.when(b_z == farthest)(lambda: pass_on(2))
            arrived(bb)
            if e == 2:
                pl.when(b_core == farthest)(z_copies[2].start)
            spread(bb)
        products(chunk, e)

    def sums(chunk):
        seconds(chunk)
        make(chunk, 2)
        for u in range(2):
            for way in range(2):
                fars[chunk, way, u] = send(
                    part[chunk].at[2, u, way],
                    far_in[chunk].at[way, u],
                    far_send.at[chunk, way, u],
                    far_recv.at[chunk, way, u],
                    along_y(ends[way]),
                )
        if chunk == 0:
            pl.when(b_z != farthest)(lambda: pass_on(2))
        for way in range(2):
            make(chunk, ends[way])
            for u in range(2):
                near(chunk, way, u, 1 - way)
        make(chunk, 0)

    def add_far(chunk):
        for u in range(2):
            for way in range(2):
                fars[chunk, way, u].wait_recv()
                part[chunk][ends[way], u, way] += far_in[chunk][way, u]
                near(chunk, way, u, way)

    def finish(chunk):
        for u in range(2):
            for way in range(2):
                for w in range(2):
                    nears[chunk, way, u, w].wait_recv()
            part[chunk][0, u] += near_in[chunk][0, u] + near_in[chunk][1, u]
            for other in range(2):
                zz = lax.rem(zh + other, 2)
                for row in range(2):
                    start = pl.multiple_of((zz * 2 + row) * 32, 32)
                    src = part[chunk].at[0, u, :, :, pl.ds(start, 32)]
                    dst = last_in[chunk].at[u, c, zh]
                    copy = pltpu.make_async_remote_copy(
                        src_ref=src,
                        dst_ref=dst,
                        send_sem=last_send.at[chunk, u, other, row],
                        recv_sem=last_recv.at[chunk, u, c, zh],
                        device_id=at(y, x, zz, row, zl),
                        device_id_type=MESH,
                    )
                    if other == 0:
                        here = jnp.logical_and(row == zl, zl == c)
                        own = pltpu.make_async_copy(src, dst, last_own.at[chunk, u])
                        lasts[chunk, u, row] = (here, copy, own)
                        pl.when(jnp.logical_not(here))(copy.start)
                        pl.when(here)(own.start)
                    else:
                        copy.start()
                        sent.append(copy)

    scale = [np.float32(1.0 / np.sqrt(np.float32(SAMPLES - k))) for k in range(1, LAGS + 1)]

    def write(chunk):
        first, count = CHUNKS[chunk]
        for u in range(2):
            for row in range(2):
                here, copy, own = lasts[chunk, u, row]
                pl.when(jnp.logical_not(here))(copy.wait_send)
                pl.when(here)(own.wait)
            for cc in range(2):
                for hh in range(2):
                    mine = jnp.logical_and(zl == c, jnp.logical_and(cc == c, hh == zh))
                    place = last_in[chunk].at[u, cc, hh]
                    copy = pltpu.make_async_remote_copy(
                        src_ref=place,
                        dst_ref=place,
                        send_sem=last_send.at[chunk, u, 0, 0],
                        recv_sem=last_recv.at[chunk, u, cc, hh],
                        device_id=other_z,
                        device_id_type=MESH,
                    )
                    pl.when(jnp.logical_not(mine))(copy.wait_recv)
            for cc in range(2):
                for q in range(count):
                    channels = lax.rem(x + first + q, 4)
                    lanes = pl.ds(pl.multiple_of(cc * 4 * LANES + channels * LANES, LANES), LANES)
                    piece = slice(q * LANES, (q + 1) * LANES)
                    for w in range(2):
                        for i in range(2):
                            k = u * 4 + w * 2 + i
                            total = last_in[chunk][u, cc, 0, w, i, :, piece] + last_in[chunk][u, cc, 1, w, i, :, piece]
                            out_ref[:, k, lanes] = total * scale[k]

    sums(0)
    pl.semaphore_signal(ready, inc=1, device_id=other_half, device_id_type=MESH)
    add_far(0)
    for copy in rest:
        copy.wait_recv()
    sums(1)
    pl.semaphore_wait(ready, 1)
    finish(0)
    add_far(1)
    write(0)
    finish(1)
    write(1)
    for copy in sent:
        copy.wait_send()


def shards(strain):
    dma, vmem = pltpu.SemaphoreType.DMA, pltpu.VMEM
    n = len(CHUNKS)
    return pl.pallas_call(
        kernel,
        out_shape=jax.ShapeDtypeStruct((32, LAGS, 8 * LANES), F32),
        in_specs=[pl.BlockSpec(memory_space=pl.ANY)],
        out_specs=pl.BlockSpec(memory_space=pltpu.VMEM),
        scratch_shapes=[
            vmem((4, 4, LEN, LANES), F32),
            vmem((4, 4, LEN + LAGS, LANES), F32),
            vmem((4, LAGS, LANES), F32),
            vmem((4, LAGS, LANES), F32),
            vmem((LAGS, LANES), F32),
            vmem((4, LAGS, LANES), F32),
            vmem((4, LANES, (2 * LAGS - 1) * DEEP), BF16),
            vmem((4, LANES, (2 * LAGS - 1) * DEEP), BF16),
            vmem((LAGS * DEEP, max(WIDTHS)), BF16),
            vmem((LAGS * DEEP, max(WIDTHS)), BF16),
            [vmem((4, 2, 2, 2, LANES, w), F32) for w in WIDTHS],
            [vmem((2, 2, 2, LANES, w), F32) for w in WIDTHS],
            [vmem((2, 2, 2, 2, LANES, w), F32) for w in WIDTHS],
            [vmem((2, 2, 2, 2, 2, 32, w), F32) for w in WIDTHS],
            dma((4,)), dma((5,)), dma((4,)), dma((4,)), dma((1,)), dma((2,)), dma((2,)), dma((12,)), dma((12,)),
            dma((5,)), dma((5,)), dma((2, 5)), dma((2, 5)), dma((n, 2, 2)), dma((n, 2, 2)),
            dma((n, 2, 2, 2)), dma((n, 2, 2, 2)), dma((n, 2, 2, 2)), dma((n, 2, 2, 2)), dma((n, 2)),
            pltpu.SemaphoreType.REGULAR,
        ],
        compiler_params=pltpu.CompilerParams(
            collective_id=0, has_side_effects=True, vmem_limit_bytes=60 * 2**20
        ),
        cost_estimate=pl.CostEstimate(flops=3 * 2 * 8 * 512 * 512 * 3072, bytes_accessed=2**22, transcendentals=0),
    )(strain)


def solution(mesh):
    placed = (P("tm", ("row", "col")),)
    return jax.shard_map(
        shards, mesh=mesh, in_specs=placed, out_specs=P(("tm", "row"), None, "col"), check_vma=False
    )
```

```python
import jax
import jax.numpy as jnp
import numpy as np
from jax import lax
from jax.experimental import pallas as pl
from jax.experimental.pallas import tpu as pltpu
from jax.sharding import PartitionSpec as P

MESH = pl.DeviceIdType.MESH
LAGS = 8
SAMPLES = 24576
LEN = 768
LANES = 128
PER = LEN // LAGS
DEEP = 4 * PER
WIDE = 2 * LANES
F32 = jnp.float32
BF16 = jnp.bfloat16


def halves(v):
    hi = v.astype(BF16)
    return hi, (v - hi.astype(F32)).astype(BF16)


def kernel(
    s_ref, out_ref, blocks, firsts, heads, heads_z, head_y, tails, x_hi, x_lo, y_hi, y_lo, part, swap_in, far_in, near_in, last_in,
    load_sem, own_sem, fan_send, fan_recv, fan_own, head_send, head_recv, ring_send, ring_recv, z_send, z_recv,
    core_send, core_recv, swap_send, swap_recv, far_send, far_recv, near_send, near_recv, last_send, last_recv, last_own, ready,
):
    tm, zl, c = lax.axis_index("tm"), lax.axis_index("row"), lax.axis_index("col")
    y, x, zh = lax.div(tm, 8), lax.rem(lax.div(tm, 2), 4), lax.rem(tm, 2)
    b = zl * 2 + c
    b_z, b_core, b_both = (1 - zl) * 2 + c, zl * 2 + 1 - c, (1 - zl) * 2 + 1 - c

    def at(yy, xx, zz, row, col):
        return (lax.rem(yy, 4) * 8 + lax.rem(xx, 4) * 2 + zz, row, col)

    def along_x(d):
        return at(y, x + d, zh, zl, c)

    def along_y(d):
        return at(y + d, x, zh, zl, c)

    other_z = (tm, 1 - zl, c)
    other_core = (tm, zl, 1 - c)
    other_half = at(y, x, 1 - zh, zl, c)

    barrier = pltpu.get_barrier_semaphore()
    peers = [along_x(1), along_x(3), along_x(2), along_y(1), along_y(3), other_z, other_core, other_half]
    for peer in peers:
        pl.semaphore_signal(barrier, inc=1, device_id=peer, device_id_type=MESH)

    loads = []
    for q in (1, 3, 2, 0):
        lanes = pl.ds(pl.multiple_of(lax.rem(x + q, 4) * LANES, LANES), LANES)
        loads.append(pltpu.make_async_copy(s_ref.at[:, lanes], blocks.at[0, q], load_sem.at[q]))
        loads[-1].start()
    for load in loads:
        load.wait()
    pl.semaphore_wait(barrier, len(peers))

    sent = []

    def send(src, dst, send_sem, recv_sem, device):
        copy = pltpu.make_async_remote_copy(
            src_ref=src, dst_ref=dst, send_sem=send_sem, recv_sem=recv_sem, device_id=device, device_id_type=MESH
        )
        copy.start()
        sent.append(copy)
        return copy

    whole = pl.ds(0, LEN)
    parts = (pl.ds(0, LEN // 2), pl.ds(LEN // 2, LEN // 2))

    def ring(n, way, d, q, rows=whole):
        return send(
            blocks.at[d, q, rows],
            blocks.at[(d - way) % 4, (q - way) % 4, rows],
            ring_send.at[n],
            ring_recv.at[n],
            along_x(way % 4),
        )

    fans = []
    for d in range(1, 4):
        fans.append(
            send(blocks.at[0, d, pl.ds(0, LAGS)], heads.at[x], fan_send.at[4 - d], fan_recv.at[4 - d], along_x(d))
        )
    fan_mine = pltpu.make_async_copy(blocks.at[0, 0, pl.ds(0, LAGS)], heads.at[x], fan_own.at[0])
    fan_mine.start()

    left_0, right_0 = [], []
    for h in range(2):
        left_0.append(ring(h, 1, 0, 1, parts[h]))
        right_0.append(ring(2 + h, -1, 0, 3, parts[h]))

    z_copies, core_copies, own_copies = {}, {}, {}
    tail = pl.ds(LEN, LAGS)
    farthest = lax.rem(y + 2, 4)

    def cross(d, n, rows):
        z_copies[n] = pltpu.make_async_remote_copy(
            src_ref=blocks.at[d, 0, rows],
            dst_ref=firsts.at[b, d, rows],
            send_sem=z_send.at[n],
            recv_sem=z_recv.at[n],
            device_id=other_z,
            device_id_type=MESH,
        )
        sent.append(z_copies[n])
        if d == 2:
            pl.when(b_core != farthest)(z_copies[n].start)
        else:
            z_copies[n].start()
        core_copies[n] = send(
            blocks.at[d, 0, rows], firsts.at[b, d, rows], core_send.at[0, n], core_recv.at[0, n], other_core
        )
        own_copies[n] = pltpu.make_async_copy(blocks.at[d, 0, rows], firsts.at[b, d, rows], own_sem.at[n])
        own_copies[n].start()

    def pass_on(n):
        z_copies[n].wait_recv()
        core_copies[6 + n].start()

    def late(do):
        for n in (2, 4):
            do(n)

    for n in range(6):
        d, rows = (2, parts[n // 4]) if n in (2, 4) else (n, whole)
        src = firsts.at[b_z, :, tail] if n == 5 else firsts.at[b_z, d, rows]
        core_copies[6 + n] = pltpu.make_async_remote_copy(
            src_ref=src,
            dst_ref=src,
            send_sem=core_send.at[1, n],
            recv_sem=core_recv.at[1, n],
            device_id=other_core,
            device_id_type=MESH,
        )
        sent.append(core_copies[6 + n])

    fan_mine.wait()
    for copy in fans:
        copy.wait_recv()
    over_z = send(heads, heads_z, head_send.at[0], head_recv.at[0], other_half)
    cross(0, 0, whole)

    def seconds(first, q, d):
        cols = slice(q * LANES, (q + 1) * LANES)
        for r in range(LAGS):
            hi, lo = halves(blocks[d, first + q, pl.ds(r, PER, stride=LAGS), :])
            to = pl.ds(pl.multiple_of(r * DEEP + d * PER, PER), PER)
            y_hi[to, cols] = hi
            y_lo[to, cols] = lo

    left_0[0].wait_recv()
    right_0[0].wait_recv()
    left_1, right_1, from_far, far_1 = [], [], [], []
    for h in range(2):
        left_1.append(ring(4 + h, 1, 0, 2, parts[h]))
        right_1.append(ring(6 + h, -1, 0, 0, parts[h]))
    left_0[1].wait_recv()
    cross(3, 3, whole)
    right_0[1].wait_recv()
    cross(1, 1, whole)
    over_z.wait_recv()
    over_y = send(heads_z.at[0], head_y, head_send.at[1], head_recv.at[1], along_y(3))
    seconds(0, 0, 0)
    seconds(0, 1, 0)
    for h in range(2):
        left_1[h].wait_recv()
        from_far.append(ring(8 + h, 1, 3, 1, parts[h]))
        far_1.append(ring(10 + h, -1, 1, 0, parts[h]))
    over_y.wait_recv()
    for d in range(4):
        place = lax.rem(x + d, 4)
        beyond = jnp.where(y == 3, jnp.zeros((LAGS, LANES), F32), head_y[...])
        after = jnp.where(place == 3, beyond, heads_z[lax.rem(place + 1, 4)])
        tails[d] = jnp.where(zh == 0, heads_z[place], after)
    z_copies[5] = send(tails, firsts.at[b, :, tail], z_send.at[5], z_recv.at[5], other_z)
    core_copies[5] = send(tails, firsts.at[b, :, tail], core_send.at[0, 5], core_recv.at[0, 5], other_core)
    own_copies[5] = pltpu.make_async_copy(tails, firsts.at[b, :, tail], own_sem.at[5])
    own_copies[5].start()
    pass_on(0)
    for h in range(2):
        right_1[h].wait_recv()
    seconds(0, 0, 3)
    seconds(0, 1, 3)
    seconds(0, 0, 1)
    seconds(0, 1, 1)
    for h in range(2):
        from_far[h].wait_recv()
        cross(2, 2 + 2 * h, parts[h])
    rest = [ring(12, 1, 0, 3), ring(13, -1, 0, 1), ring(14, -1, 1, 1), ring(15, 1, 0, 0), ring(16, -1, 0, 2), ring(17, 1, 3, 0)]
    for h in range(2):
        far_1[h].wait_recv()
    seconds(0, 0, 2)
    seconds(0, 1, 2)
    for n in (3, 1, 5):
        pass_on(n)

    def arrived(bb):
        @pl.when(bb == b)
        def _():
            for n in range(6):
                own_copies[n].wait()

        @pl.when(bb == b_core)
        def _():
            for n in range(6):
                core_copies[n].wait_recv()

        @pl.when(bb == b_both)
        def _():
            for n in range(6):
                core_copies[6 + n].wait_recv()

    def spread(bb):
        for m in range(1, 2 * LAGS):
            v = jnp.concatenate([firsts[bb, d, pl.ds(m, PER, stride=LAGS), :] for d in range(4)], axis=0)
            hi, lo = halves(v.T)
            lanes = slice((m - 1) * DEEP, m * DEEP)
            x_hi[bb, :, lanes] = hi
            x_lo[bb, :, lanes] = lo

    ends = (1, 3)
    lanes = (pl.ds(0, LANES), pl.ds(LANES, LANES))
    mine = pl.ds(pl.multiple_of(zh * 64, 64), 64)
    yours = pl.ds(pl.multiple_of((1 - zh) * 64, 64), 64)
    span = (pl.ds(0, LANES), mine)

    def remote(src, dst, send_sem, recv_sem, device):
        return pltpu.make_async_remote_copy(
            src_ref=src, dst_ref=dst, send_sem=send_sem, recv_sem=recv_sem, device_id=device, device_id_type=MESH
        )

    def swap(chunk, e, n):
        if e in ends:
            src, dst = part.at[chunk, e, :, n, :, yours, lanes[1]], swap_in.at[chunk, e, :, n]
        else:
            src, dst = part.at[chunk, e, n, :, :, yours, lanes[1]], swap_in.at[chunk, e, n]
        return remote(src, dst, swap_send.at[chunk, e, n], swap_recv.at[chunk, e, n], other_half)

    def add_swap(chunk, e, n):
        swap(chunk, e, n).wait_recv()
        if e in ends:
            part[chunk, e, :, n, :, mine, lanes[1]] += swap_in[chunk, e, :, n]
        else:
            part[chunk, e, n, :, :, mine, lanes[1]] += swap_in[chunk, e, n]

    def far(chunk, f, way, u):
        return remote(
            part.at[chunk, 2, u, way, :, span[f], lanes[f]],
            far_in[f].at[chunk, way, u],
            far_send.at[chunk, f, way, u],
            far_recv.at[chunk, f, way, u],
            along_y(ends[way]),
        )

    def near(chunk, f, way, u, w):
        return remote(
            part.at[chunk, ends[way], u, w, :, span[f], lanes[f]],
            near_in[f].at[chunk, way, u, w],
            near_send.at[chunk, f, way, u, w],
            near_recv.at[chunk, f, way, u, w],
            along_y(ends[way]),
        )

    def pure(chunk, f, way):
        for u in range(2):
            near(chunk, f, way, u, 1 - way).start()

    def add_far(chunk, f):
        for u in range(2):
            for way in range(2):
                far(chunk, f, way, u).wait_recv()
                part[chunk, ends[way], u, way, :, span[f], lanes[f]] += far_in[f][chunk, way, u]
                near(chunk, f, way, u, way).start()

    def after(chunk, j):
        if j < 2:
            swap(chunk, 2, j).start()
            for way in range(2):
                far(chunk, 0, way, j).start()
        elif j < 6:
            way = j % 2
            n = 1 - way if j < 4 else way
            swap(chunk, ends[way], n).start()
            if j < 4:
                pure(chunk, 0, way)
        else:
            swap(chunk, 0, j - 6).start()
        if j == 3:
            for u in range(2):
                add_swap(chunk, 2, u)
                for way in range(2):
                    far(chunk, 1, way, u).start()
        if j == 5:
            add_far(chunk, 0)
            for way in range(2):
                add_swap(chunk, ends[way], 1 - way)
                pure(chunk, 1, way)
        if j == 7:
            for way in range(2):
                add_swap(chunk, ends[way], way)
            add_far(chunk, 1)

    def before(s):
        if s == 0:
            pl.when(b_z == farthest)(lambda: late(pass_on))
            arrived(farthest)
            pl.when(b_core == farthest)(lambda: late(lambda n: z_copies[n].start()))
        if s == 2:
            pl.when(b_z != farthest)(lambda: late(pass_on))
            arrived(lax.rem(y + 1, 4))
        if s == 3:
            arrived(lax.rem(y + 3, 4))
        if s == 6:
            arrived(y)
        if s == 8:
            pl.semaphore_signal(ready, inc=1, device_id=other_half, device_id_type=MESH)
            for copy in rest:
                copy.wait_recv()

            def one(d, carry):
                for q in range(2):
                    seconds(2, q, d)
                return carry

            lax.fori_loop(0, 4, one, 0)

    def step(s, carry):
        chunk, j = lax.div(s, 8), lax.rem(s, 8)
        odd = lax.rem(j, 2)
        e = jnp.where(j < 2, 2, jnp.where(j < 6, 1 + 2 * odd, 0))
        bb = lax.rem(y + e, 4)
        for i in (0, 2, 3, 6, 8):
            pl.when(s == i)(lambda i=i: before(i))
        pl.when(jnp.logical_or(s == 0, jnp.logical_or(jnp.logical_or(s == 2, s == 3), s == 6)))(lambda: spread(bb))

        by_way = jnp.logical_and(j >= 2, j < 6)
        w = jnp.where(j < 4, 1 - odd, odd)
        pairs = [
            (jnp.where(by_way, 0, odd), jnp.where(by_way, w, 0)),
            (jnp.where(by_way, 1, odd), jnp.where(by_way, w, 1)),
        ]
        for u, w in pairs:
            pass

        def dots(n, carry):
            starts = [
                pl.multiple_of( (u * 4 + w * 2 + i) * DEEP, LANES) for u, w in pairs for i in range(2)
            ]
            lhs_hi = jnp.concatenate([x_hi[bb, :, pl.ds(start, LAGS * DEEP)] for start in starts], axis=0)
            lhs_lo = jnp.concatenate([x_lo[bb, :, pl.ds(start, LAGS * DEEP)] for start in starts], axis=0)
            deep = pl.ds(0, LAGS * DEEP)
            rhs_hi, rhs_lo = y_hi[deep, :], y_lo[deep, :]
            got = jnp.dot(lhs_hi, rhs_hi, preferred_element_type=F32)
            got += jnp.dot(lhs_lo, rhs_hi, preferred_element_type=F32)
            got += jnp.dot(lhs_hi, rhs_lo, preferred_element_type=F32)
            got = got.reshape(2, 2, LANES, WIDE)
            for n, (u, w) in enumerate(pairs):
                part[chunk, e, u, w] = got[n]
            return carry

        dots(0, 0)
        for i in range(8):
            pl.when(j == i)(lambda i=i: after(chunk, i))

        @pl.when(s == 10)
        def _():
            pl.semaphore_wait(ready, 1)
            finish(0, 0)
            finish(0, 1)

        return carry

    def total(chunk, f, u):
        for way in range(2):
            for w in range(2):
                near(chunk, f, way, u, w).wait_recv()
        part[chunk, 0, u, :, :, span[f], lanes[f]] += near_in[f][chunk, 0, u] + near_in[f][chunk, 1, u]

    def deal(chunk, f, u, other, row):
        zz = lax.rem(zh + other, 2)
        src = part.at[chunk, 0, u, :, :, pl.ds(pl.multiple_of((zz * 2 + row) * 32, 32), 32), lanes[f]]
        dst = last_in[0].at[chunk, u, c, zh] if f == 0 else last_in[1].at[chunk, u, c]
        recv_sem = last_recv.at[chunk, u, c, zh] if f == 0 else last_recv.at[chunk, u, c, 2]
        copy = remote(src, dst, last_send.at[chunk, f, u, other, row], recv_sem, at(y, x, zz, row, zl))
        return copy, pltpu.make_async_copy(src, dst, last_own.at[chunk, f, u]) if other == 0 else None

    def finish(chunk, f):
        for u in range(2):
            if f == 1:
                add_swap(chunk, 0, u)
            total(chunk, f, u)
            for other in range(2 - f):
                for row in range(2):
                    copy, own = deal(chunk, f, u, other, row)
                    if other == 0:
                        here = jnp.logical_and(row == zl, zl == c)
                        pl.when(jnp.logical_not(here))(copy.start)
                        pl.when(here)(own.start)
                    else:
                        copy.start()

    scale = [np.float32(1.0 / np.sqrt(np.float32(SAMPLES - k))) for k in range(1, LAGS + 1)]

    def write(chunk, f):
        channels = lax.rem(x + 2 * chunk + f, 4)
        for u in range(2):
            for other in range(2 - f):
                for row in range(2):
                    copy, own = deal(chunk, f, u, other, row)
                    if other == 0:
                        here = jnp.logical_and(row == zl, zl == c)
                        pl.when(jnp.logical_not(here))(copy.wait_send)
                        pl.when(here)(own.wait)
                    else:
                        copy.wait_send()
            for cc in range(2):
                for hh in range(2) if f == 0 else (2,):
                    same = jnp.logical_and(zl == c, cc == c)
                    if f == 0:
                        same = jnp.logical_and(same, hh == zh)
                    place = last_in[0].at[chunk, u, cc, hh] if f == 0 else last_in[1].at[chunk, u, cc]
                    copy = pltpu.make_async_remote_copy(
                        src_ref=place,
                        dst_ref=place,
                        send_sem=last_send.at[chunk, f, u, 0, 0],
                        recv_sem=last_recv.at[chunk, u, cc, hh],
                        device_id=other_z,
                        device_id_type=MESH,
                    )
                    pl.when(jnp.logical_not(same))(copy.wait_recv)
            for cc in range(2):
                to = pl.ds(pl.multiple_of(cc * 4 * LANES + channels * LANES, LANES), LANES)
                for w in range(2):
                    for i in range(2):
                        k = u * 4 + w * 2 + i
                        if f == 0:
                            got = last_in[0][chunk, u, cc, 0, w, i] + last_in[0][chunk, u, cc, 1, w, i]
                        else:
                            got = last_in[1][chunk, u, cc, w, i]
                        out_ref[:, k, to] = got * scale[k]

    lax.fori_loop(0, 16, step, 0)
    finish(1, 0)
    write(0, 0)
    write(0, 1)
    finish(1, 1)
    write(1, 0)
    write(1, 1)
    for copy in sent:
        copy.wait_send()

    def drain(chunk, carry):
        for n in range(2):
            for e in range(4):
                swap(chunk, e, n).wait_send()
        for f in range(2):
            for way in range(2):
                for u in range(2):
                    far(chunk, f, way, u).wait_send()
                    for w in range(2):
                        near(chunk, f, way, u, w).wait_send()
        return carry

    lax.fori_loop(0, 2, drain, 0)


def shards(strain):
    dma, vmem = pltpu.SemaphoreType.DMA, pltpu.VMEM
    return pl.pallas_call(
        kernel,
        out_shape=jax.ShapeDtypeStruct((32, LAGS, 8 * LANES), F32),
        in_specs=[pl.BlockSpec(memory_space=pl.ANY)],
        out_specs=pl.BlockSpec(memory_space=pltpu.VMEM),
        scratch_shapes=[
            vmem((4, 4, LEN, LANES), F32),
            vmem((4, 4, LEN + LAGS, LANES), F32),
            vmem((4, LAGS, LANES), F32),
            vmem((4, LAGS, LANES), F32),
            vmem((LAGS, LANES), F32),
            vmem((4, LAGS, LANES), F32),
            vmem((4, LANES, (2 * LAGS - 1) * DEEP), BF16),
            vmem((4, LANES, (2 * LAGS - 1) * DEEP), BF16),
            vmem((LAGS * DEEP, WIDE), BF16),
            vmem((LAGS * DEEP, WIDE), BF16),
            vmem((2, 4, 2, 2, 2, LANES, WIDE), F32),
            vmem((2, 4, 2, 2, 2, 64, LANES), F32),
            [vmem((2, 2, 2, 2, n, LANES), F32) for n in (LANES, 64)],
            [vmem((2, 2, 2, 2, 2, n, LANES), F32) for n in (LANES, 64)],
            [vmem((2, 2, 2, 2, 2, 2, 32, LANES), F32), vmem((2, 2, 2, 2, 2, 32, LANES), F32)],
            dma((4,)), dma((6,)), dma((4,)), dma((4,)), dma((1,)), dma((2,)), dma((2,)), dma((18,)), dma((18,)),
            dma((6,)), dma((6,)), dma((2, 6)), dma((2, 6)), dma((2, 4, 2)), dma((2, 4, 2)),
            dma((2, 2, 2, 2)), dma((2, 2, 2, 2)), dma((2, 2, 2, 2, 2)), dma((2, 2, 2, 2, 2)),
            dma((2, 2, 2, 2, 2)), dma((2, 2, 2, 3)), dma((2, 2, 2)),
            pltpu.SemaphoreType.REGULAR,
        ],
        compiler_params=pltpu.CompilerParams(
            collective_id=0, has_side_effects=True, vmem_limit_bytes=60 * 2**20
        ),
        cost_estimate=pl.CostEstimate(flops=3 * 2 * 8 * 512 * 512 * 3072, bytes_accessed=2**22, transcendentals=0),
    )(strain)


def solution(mesh):
    placed = (P("tm", ("row", "col")),)
    return jax.shard_map(
        shards, mesh=mesh, in_specs=placed, out_specs=P(("tm", "row"), None, "col"), check_vma=False
    )
```

```python
import jax
import jax.numpy as jnp
import numpy as np
from jax import lax
from jax.experimental import pallas as pl
from jax.experimental.pallas import tpu as pltpu
from jax.sharding import PartitionSpec as P

MESH = pl.DeviceIdType.MESH
LAGS = 8
SAMPLES = 24576
LEN = 768
LANES = 128
PER = LEN // LAGS
DEEP = 4 * PER
WIDE = 2 * LANES
STRAIGHT = ((1, 1),)
F32 = jnp.float32
BF16 = jnp.bfloat16


def halves(v):
    hi = v.astype(BF16)
    return hi, (v - hi.astype(F32)).astype(BF16)


def kernel(
    s_ref, out_ref, blocks, firsts, heads, heads_z, head_y, tails, x_hi, x_lo, y_hi, y_lo, part, swap_in, far_in, near_in, last_in,
    load_sem, own_sem, fan_send, fan_recv, fan_own, head_send, head_recv, ring_send, ring_recv, z_send, z_recv,
    core_send, core_recv, swap_send, swap_recv, far_send, far_recv, near_send, near_recv, last_send, last_recv, last_own, ready,
):
    tm, zl, c = lax.axis_index("tm"), lax.axis_index("row"), lax.axis_index("col")
    y, x, zh = lax.div(tm, 8), lax.rem(lax.div(tm, 2), 4), lax.rem(tm, 2)
    b = zl * 2 + c
    b_z, b_core, b_both = (1 - zl) * 2 + c, zl * 2 + 1 - c, (1 - zl) * 2 + 1 - c

    def at(yy, xx, zz, row, col):
        return (lax.rem(yy, 4) * 8 + lax.rem(xx, 4) * 2 + zz, row, col)

    def along_x(d):
        return at(y, x + d, zh, zl, c)

    def along_y(d):
        return at(y + d, x, zh, zl, c)

    other_z = (tm, 1 - zl, c)
    other_core = (tm, zl, 1 - c)
    other_half = at(y, x, 1 - zh, zl, c)

    barrier = pltpu.get_barrier_semaphore()
    peers = [along_x(1), along_x(3), along_x(2), along_y(1), along_y(3), other_z, other_core, other_half]
    for peer in peers:
        pl.semaphore_signal(barrier, inc=1, device_id=peer, device_id_type=MESH)

    loads = []
    for q in (1, 3, 2, 0):
        lanes = pl.ds(pl.multiple_of(lax.rem(x + q, 4) * LANES, LANES), LANES)
        loads.append(pltpu.make_async_copy(s_ref.at[:, lanes], blocks.at[0, q], load_sem.at[q]))
        loads[-1].start()
    for load in loads:
        load.wait()
    pl.semaphore_wait(barrier, len(peers))

    sent = []

    def send(src, dst, send_sem, recv_sem, device):
        copy = pltpu.make_async_remote_copy(
            src_ref=src, dst_ref=dst, send_sem=send_sem, recv_sem=recv_sem, device_id=device, device_id_type=MESH
        )
        copy.start()
        sent.append(copy)
        return copy

    whole = pl.ds(0, LEN)
    parts = (pl.ds(0, LEN // 2), pl.ds(LEN // 2, LEN // 2))

    def ring(n, way, d, q, rows=whole):
        return send(
            blocks.at[d, q, rows],
            blocks.at[(d - way) % 4, (q - way) % 4, rows],
            ring_send.at[n],
            ring_recv.at[n],
            along_x(way % 4),
        )

    fans = []
    for d in range(1, 4):
        fans.append(
            send(blocks.at[0, d, pl.ds(0, LAGS)], heads.at[x], fan_send.at[4 - d], fan_recv.at[4 - d], along_x(d))
        )
    fan_mine = pltpu.make_async_copy(blocks.at[0, 0, pl.ds(0, LAGS)], heads.at[x], fan_own.at[0])
    fan_mine.start()

    left_0, right_0 = [], []
    for h in range(2):
        left_0.append(ring(h, 1, 0, 1, parts[h]))
        right_0.append(ring(2 + h, -1, 0, 3, parts[h]))

    z_copies, core_copies, own_copies = {}, {}, {}
    tail = pl.ds(LEN, LAGS)
    farthest = lax.rem(y + 2, 4)
    later = jnp.logical_or(b_core == farthest, b == y)
    later_z = jnp.logical_or(b_both == farthest, b_z == y)

    def cross(d, n, rows):
        z_copies[n] = pltpu.make_async_remote_copy(
            src_ref=blocks.at[d, 0, rows],
            dst_ref=firsts.at[b, d, rows],
            send_sem=z_send.at[n],
            recv_sem=z_recv.at[n],
            device_id=other_z,
            device_id_type=MESH,
        )
        sent.append(z_copies[n])
        if d == 2:
            pl.when(jnp.logical_not(later))(z_copies[n].start)
        else:
            z_copies[n].start()
        core_copies[n] = send(
            blocks.at[d, 0, rows], firsts.at[b, d, rows], core_send.at[0, n], core_recv.at[0, n], other_core
        )
        own_copies[n] = pltpu.make_async_copy(blocks.at[d, 0, rows], firsts.at[b, d, rows], own_sem.at[n])
        own_copies[n].start()

    def pass_on(n):
        z_copies[n].wait_recv()
        core_copies[6 + n].start()

    def late(do):
        for n in (2, 4):
            do(n)

    for n in range(6):
        d, rows = (2, parts[n // 4]) if n in (2, 4) else (n, whole)
        src = firsts.at[b_z, :, tail] if n == 5 else firsts.at[b_z, d, rows]
        core_copies[6 + n] = pltpu.make_async_remote_copy(
            src_ref=src,
            dst_ref=src,
            send_sem=core_send.at[1, n],
            recv_sem=core_recv.at[1, n],
            device_id=other_core,
            device_id_type=MESH,
        )
        sent.append(core_copies[6 + n])

    fan_mine.wait()
    for copy in fans:
        copy.wait_recv()
    over_z = send(heads, heads_z, head_send.at[0], head_recv.at[0], other_half)
    cross(0, 0, whole)

    def seconds(first, q, d):
        cols = slice(q * LANES, (q + 1) * LANES)
        for r in range(LAGS):
            hi, lo = halves(blocks[d, first + q, pl.ds(r, PER, stride=LAGS), :])
            to = pl.ds(pl.multiple_of(r * DEEP + d * PER, PER), PER)
            y_hi[to, cols] = hi
            y_lo[to, cols] = lo

    left_0[0].wait_recv()
    right_0[0].wait_recv()
    left_1, right_1, from_far, far_1 = [], [], [], []
    for h in range(2):
        left_1.append(ring(4 + h, 1, 0, 2, parts[h]))
        right_1.append(ring(6 + h, -1, 0, 0, parts[h]))
    left_0[1].wait_recv()
    cross(3, 3, whole)
    right_0[1].wait_recv()
    cross(1, 1, whole)
    over_z.wait_recv()
    over_y = send(heads_z.at[0], head_y, head_send.at[1], head_recv.at[1], along_y(3))
    seconds(0, 0, 0)
    seconds(0, 1, 0)
    for h in range(2):
        left_1[h].wait_recv()
        from_far.append(ring(8 + h, 1, 3, 1, parts[h]))
        far_1.append(ring(10 + h, -1, 1, 0, parts[h]))
    over_y.wait_recv()
    for d in range(4):
        place = lax.rem(x + d, 4)
        beyond = jnp.where(y == 3, jnp.zeros((LAGS, LANES), F32), head_y[...])
        after = jnp.where(place == 3, beyond, heads_z[lax.rem(place + 1, 4)])
        tails[d] = jnp.where(zh == 0, heads_z[place], after)
    z_copies[5] = send(tails, firsts.at[b, :, tail], z_send.at[5], z_recv.at[5], other_z)
    core_copies[5] = send(tails, firsts.at[b, :, tail], core_send.at[0, 5], core_recv.at[0, 5], other_core)
    own_copies[5] = pltpu.make_async_copy(tails, firsts.at[b, :, tail], own_sem.at[5])
    own_copies[5].start()
    pass_on(0)
    for h in range(2):
        right_1[h].wait_recv()
    seconds(0, 0, 3)
    seconds(0, 1, 3)
    seconds(0, 0, 1)
    seconds(0, 1, 1)
    for h in range(2):
        from_far[h].wait_recv()
        cross(2, 2 + 2 * h, parts[h])
    rest = [ring(12, 1, 0, 3), ring(13, -1, 0, 1), ring(14, -1, 1, 1), ring(15, 1, 0, 0), ring(16, -1, 0, 2), ring(17, 1, 3, 0)]
    for h in range(2):
        far_1[h].wait_recv()
    seconds(0, 0, 2)
    seconds(0, 1, 2)
    for n in (3, 1, 5):
        pass_on(n)

    def arrived(bb):
        @pl.when(bb == b)
        def _():
            for n in range(6):
                own_copies[n].wait()

        @pl.when(bb == b_core)
        def _():
            for n in range(6):
                core_copies[n].wait_recv()

        @pl.when(bb == b_both)
        def _():
            for n in range(6):
                core_copies[6 + n].wait_recv()

    def spread(bb):
        for m in range(1, 2 * LAGS):
            v = jnp.concatenate([firsts[bb, d, pl.ds(m, PER, stride=LAGS), :] for d in range(4)], axis=0)
            hi, lo = halves(v.T)
            lanes = slice((m - 1) * DEEP, m * DEEP)
            x_hi[bb, :, lanes] = hi
            x_lo[bb, :, lanes] = lo

    ends = (1, 3)
    lanes = (pl.ds(0, LANES), pl.ds(LANES, LANES))
    mine = pl.ds(pl.multiple_of(zh * 64, 64), 64)
    yours = pl.ds(pl.multiple_of((1 - zh) * 64, 64), 64)

    def remote(src, dst, send_sem, recv_sem, device):
        return pltpu.make_async_remote_copy(
            src_ref=src, dst_ref=dst, send_sem=send_sem, recv_sem=recv_sem, device_id=device, device_id_type=MESH
        )

    def whole_sums(chunk, f, u):
        return f == 0 or (chunk, u) in STRAIGHT

    def swap(chunk, e, n):
        if e not in ends:
            src, dst = part.at[chunk, e, n, :, :, yours, lanes[1]], swap_in.at[chunk, e, n]
        elif whole_sums(chunk, 1, 1):
            src, dst = part.at[chunk, e, 0, n, :, yours, lanes[1]], swap_in.at[chunk, e, 0, n]
        else:
            src, dst = part.at[chunk, e, :, n, :, yours, lanes[1]], swap_in.at[chunk, e, :, n]
        return remote(src, dst, swap_send.at[chunk, e, n], swap_recv.at[chunk, e, n], other_half)

    def add_swap(chunk, e, n):
        swap(chunk, e, n).wait_recv()
        if e not in ends:
            part[chunk, e, n, :, :, mine, lanes[1]] += swap_in[chunk, e, n]
        elif whole_sums(chunk, 1, 1):
            part[chunk, e, 0, n, :, mine, lanes[1]] += swap_in[chunk, e, 0, n]
        else:
            part[chunk, e, :, n, :, mine, lanes[1]] += swap_in[chunk, e, :, n]

    def span(chunk, f, u):
        return (pl.ds(0, LANES), pl.ds(0, LANES)) if whole_sums(chunk, f, u) else (mine, pl.ds(0, 64))

    def far(chunk, f, way, u):
        here, there = span(chunk, f, u)
        return remote(
            part.at[chunk, 2, u, way, :, here, lanes[f]],
            far_in.at[chunk, f, way, u, :, there],
            far_send.at[chunk, f, way, u],
            far_recv.at[chunk, f, way, u],
            along_y(ends[way]),
        )

    def near(chunk, f, way, u, w):
        here, there = span(chunk, f, u)
        return remote(
            part.at[chunk, ends[way], u, w, :, here, lanes[f]],
            near_in.at[chunk, f, way, u, w, :, there],
            near_send.at[chunk, f, way, u, w],
            near_recv.at[chunk, f, way, u, w],
            along_y(ends[way]),
        )

    def kinds(chunk, straight):
        return [(f, u) for f in range(2) for u in range(2) if whole_sums(chunk, f, u) == straight]

    def add_far(chunk, straight):
        for f, u in kinds(chunk, straight):
            here, there = span(chunk, f, u)
            for way in range(2):
                far(chunk, f, way, u).wait_recv()
                part[chunk, ends[way], u, way, :, here, lanes[f]] += far_in[chunk, f, way, u, :, there]
                near(chunk, f, way, u, way).start()

    def after_product(chunk, j):
        if j < 2:
            for f, u in kinds(chunk, True):
                if u == j:
                    for way in range(2):
                        far(chunk, f, way, u).start()
            if not whole_sums(chunk, 1, j):
                swap(chunk, 2, j).start()
        elif j < 6:
            way = j % 2
            n = 1 - way if j < 4 else way
            if j < 4:
                for f, u in kinds(chunk, True):
                    near(chunk, f, way, u, 1 - way).start()
            swap(chunk, ends[way], n).start()
        elif not whole_sums(chunk, 1, j - 6):
            swap(chunk, 0, j - 6).start()

    def after_step(chunk, p):
        if p == 4:
            for f, u in kinds(chunk, False):
                add_swap(chunk, 2, u)
                for way in range(2):
                    far(chunk, f, way, u).start()
        if p == 5:
            add_far(chunk, True)
        if p == 6:
            for way in range(2):
                add_swap(chunk, ends[way], 1 - way)
                for f, u in kinds(chunk, False):
                    near(chunk, f, way, u, 1 - way).start()
        if p == 7:
            for way in range(2):
                add_swap(chunk, ends[way], way)
            add_far(chunk, False)

    def before(s):
        if s == 1:
            pl.when(later)(lambda: late(lambda n: z_copies[n].start()))
        if s == 2:
            pl.when(jnp.logical_not(later_z))(lambda: late(pass_on))
        if s == 4:
            pl.when(later_z)(lambda: late(pass_on))
        if s == 8:
            pl.semaphore_signal(ready, inc=1, device_id=other_half, device_id_type=MESH)
            for copy in rest:
                copy.wait_recv()

            def one(d, carry):
                for q in range(2):
                    seconds(2, q, d)
                return carry

            lax.fori_loop(0, 4, one, 0)

    far_here = zl == lax.div(farthest, 2)
    near_first = jnp.where(far_here, 1 - lax.rem(y, 2), lax.rem(y, 2))

    def step(s, carry):
        chunk, p = lax.div(s, 8), lax.rem(s, 8)
        by_far = jnp.logical_or(far_here, chunk == 1)
        second = lax.rem(p, 2)
        near_l = jnp.where(p < 4, 2, 4) + jnp.where(second == 0, near_first, 1 - near_first)
        near_r = jnp.where(p < 2, near_first, 1 - near_first) + 2 * second + 2
        order_l = jnp.where(jnp.logical_and(p >= 2, p < 6), near_l, p)
        order_r = jnp.where(p >= 6, p, jnp.where(jnp.logical_and(p >= 2, p < 4), p - 2, near_r))
        j = jnp.where(by_far, order_l, order_r)
        odd = lax.rem(j, 2)
        e = jnp.where(j < 2, 2, jnp.where(j < 6, 1 + 2 * odd, 0))
        bb = lax.rem(y + e, 4)
        for i in (1, 2, 4, 8):
            pl.when(s == i)(lambda i=i: before(i))
        fresh = jnp.logical_or(jnp.logical_or(s == 0, s == 2), jnp.logical_or(s == 6, s == jnp.where(far_here, 3, 4)))

        @pl.when(fresh)
        def _():
            arrived(bb)
            spread(bb)

        by_way = jnp.logical_and(j >= 2, j < 6)
        w = jnp.where(j < 4, 1 - odd, odd)
        pairs = [
            (jnp.where(by_way, 0, odd), jnp.where(by_way, w, 0)),
            (jnp.where(by_way, 1, odd), jnp.where(by_way, w, 1)),
        ]
        for u, w in pairs:
            pass

        def dots(n, carry):
            starts = [
                pl.multiple_of( (u * 4 + w * 2 + i) * DEEP, LANES) for u, w in pairs for i in range(2)
            ]
            lhs_hi = jnp.concatenate([x_hi[bb, :, pl.ds(start, LAGS * DEEP)] for start in starts], axis=0)
            lhs_lo = jnp.concatenate([x_lo[bb, :, pl.ds(start, LAGS * DEEP)] for start in starts], axis=0)
            deep = pl.ds(0, LAGS * DEEP)
            rhs_hi, rhs_lo = y_hi[deep, :], y_lo[deep, :]
            got = jnp.dot(lhs_hi, rhs_hi, preferred_element_type=F32)
            got += jnp.dot(lhs_lo, rhs_hi, preferred_element_type=F32)
            got += jnp.dot(lhs_hi, rhs_lo, preferred_element_type=F32)
            got = got.reshape(2, 2, LANES, WIDE)
            for n, (u, w) in enumerate(pairs):
                part[chunk, e, u, w] = got[n]
            return carry

        dots(0, 0)
        for i in range(16):
            pl.when(jnp.logical_and(chunk == i // 8, j == i % 8))(lambda i=i: after_product(i // 8, i % 8))
        for i in (4, 5, 6, 7, 12, 13, 14, 15):
            pl.when(s == i)(lambda i=i: after_step(i // 8, i % 8))

        @pl.when(s == 10)
        def _():
            pl.semaphore_wait(ready, 1)
            finish(0, 0)
            finish(0, 1)

        return carry

    def total(chunk, f, u):
        here, there = span(chunk, f, u)
        for way in range(2):
            for w in range(2):
                near(chunk, f, way, u, w).wait_recv()
        part[chunk, 0, u, :, :, here, lanes[f]] += (
            near_in[chunk, f, 0, u, :, :, there] + near_in[chunk, f, 1, u, :, :, there]
        )

    def deals(chunk, f, u):
        straight = whole_sums(chunk, f, u)
        half = zh if straight else 0
        for other in range(2 if straight else 1):
            for row in range(2):
                zz = lax.rem(zh + other, 2)
                src = part.at[chunk, 0, u, :, :, pl.ds(pl.multiple_of((zz * 2 + row) * 32, 32), 32), lanes[f]]
                dst = last_in.at[chunk, f, u, c, half]
                copy = remote(
                    src,
                    dst,
                    last_send.at[chunk, f, u, other, row],
                    last_recv.at[chunk, f, u, c, half],
                    at(y, x, zz, row, zl),
                )
                if other == 0:
                    here = jnp.logical_and(row == zl, zl == c)
                    yield here, copy, pltpu.make_async_copy(src, dst, last_own.at[chunk, f, u])
                else:
                    yield None, copy, None

    def finish(chunk, f, units=(0, 1)):
        for u in units:
            if not whole_sums(chunk, f, u):
                add_swap(chunk, 0, u)
            total(chunk, f, u)
            for here, copy, own in deals(chunk, f, u):
                if here is None:
                    copy.start()
                else:
                    pl.when(jnp.logical_not(here))(copy.start)
                    pl.when(here)(own.start)

    scale = [np.float32(1.0 / np.sqrt(np.float32(SAMPLES - k))) for k in range(1, LAGS + 1)]

    def write(chunk, f, units=(0, 1)):
        channels = lax.rem(x + 2 * chunk + f, 4)
        for u in units:
            for here, copy, own in deals(chunk, f, u):
                if here is None:
                    copy.wait_send()
                else:
                    pl.when(jnp.logical_not(here))(copy.wait_send)
                    pl.when(here)(own.wait)
            straight = whole_sums(chunk, f, u)
            for cc in range(2):
                for hh in range(2 if straight else 1):
                    same = jnp.logical_and(zl == c, cc == c)
                    if straight:
                        same = jnp.logical_and(same, hh == zh)
                    place = last_in.at[chunk, f, u, cc, hh]
                    copy = remote(
                        place, place, last_send.at[chunk, f, u, 0, 0], last_recv.at[chunk, f, u, cc, hh], other_z
                    )
                    pl.when(jnp.logical_not(same))(copy.wait_recv)
            for cc in range(2):
                to = pl.ds(pl.multiple_of(cc * 4 * LANES + channels * LANES, LANES), LANES)
                for w in range(2):
                    for i in range(2):
                        k = u * 4 + w * 2 + i
                        got = last_in[chunk, f, u, cc, 0, w, i]
                        if straight:
                            got += last_in[chunk, f, u, cc, 1, w, i]
                        out_ref[:, k, to] = got * scale[k]

    lax.fori_loop(0, 16, step, 0)
    write(0, 0)
    write(0, 1)
    finish(1, 0)
    finish(1, 1, (1, 0))
    write(1, 0)
    write(1, 1, (1, 0))
    for copy in sent:
        copy.wait_send()

    for chunk in range(2):
        for n in range(2):
            for e in range(4):
                if e in ends or not whole_sums(chunk, 1, n):
                    swap(chunk, e, n).wait_send()
        for f in range(2):
            for way in range(2):
                for u in range(2):
                    far(chunk, f, way, u).wait_send()
                    for w in range(2):
                        near(chunk, f, way, u, w).wait_send()


def shards(strain):
    dma, vmem = pltpu.SemaphoreType.DMA, pltpu.VMEM
    return pl.pallas_call(
        kernel,
        out_shape=jax.ShapeDtypeStruct((32, LAGS, 8 * LANES), F32),
        in_specs=[pl.BlockSpec(memory_space=pl.ANY)],
        out_specs=pl.BlockSpec(memory_space=pltpu.VMEM),
        scratch_shapes=[
            vmem((4, 4, LEN, LANES), F32),
            vmem((4, 4, LEN + LAGS, LANES), F32),
            vmem((4, LAGS, LANES), F32),
            vmem((4, LAGS, LANES), F32),
            vmem((LAGS, LANES), F32),
            vmem((4, LAGS, LANES), F32),
            vmem((4, LANES, (2 * LAGS - 1) * DEEP), BF16),
            vmem((4, LANES, (2 * LAGS - 1) * DEEP), BF16),
            vmem((LAGS * DEEP, WIDE), BF16),
            vmem((LAGS * DEEP, WIDE), BF16),
            vmem((2, 4, 2, 2, 2, LANES, WIDE), F32),
            vmem((2, 4, 2, 2, 2, 64, LANES), F32),
            vmem((2, 2, 2, 2, 2, LANES, LANES), F32),
            vmem((2, 2, 2, 2, 2, 2, LANES, LANES), F32),
            vmem((2, 2, 2, 2, 2, 2, 2, 32, LANES), F32),
            dma((4,)), dma((6,)), dma((4,)), dma((4,)), dma((1,)), dma((2,)), dma((2,)), dma((18,)), dma((18,)),
            dma((6,)), dma((6,)), dma((2, 6)), dma((2, 6)), dma((2, 4, 2)), dma((2, 4, 2)),
            dma((2, 2, 2, 2)), dma((2, 2, 2, 2)), dma((2, 2, 2, 2, 2)), dma((2, 2, 2, 2, 2)),
            dma((2, 2, 2, 2, 2)), dma((2, 2, 2, 2, 2)), dma((2, 2, 2)),
            pltpu.SemaphoreType.REGULAR,
        ],
        compiler_params=pltpu.CompilerParams(
            collective_id=0, has_side_effects=True, vmem_limit_bytes=60 * 2**20
        ),
        cost_estimate=pl.CostEstimate(flops=3 * 2 * 8 * 512 * 512 * 3072, bytes_accessed=2**22, transcendentals=0),
    )(strain)


def solution(mesh):
    placed = (P("tm", ("row", "col")),)
    return jax.shard_map(
        shards, mesh=mesh, in_specs=placed, out_specs=P(("tm", "row"), None, "col"), check_vma=False
    )
```

```python
import jax
import jax.numpy as jnp
import numpy as np
from jax import lax
from jax.experimental import pallas as pl
from jax.experimental.pallas import tpu as pltpu
from jax.sharding import PartitionSpec as P

MESH = pl.DeviceIdType.MESH
LAGS = 8
SAMPLES = 24576
LEN = 768
LANES = 128
PER = LEN // LAGS
DEEP = 4 * PER
WIDE = 2 * LANES
STRAIGHT = ((1, 1),)
F32 = jnp.float32
BF16 = jnp.bfloat16


def halves(v):
    hi = v.astype(BF16)
    return hi, (v - hi.astype(F32)).astype(BF16)


def kernel(
    s_ref, out_ref, blocks, firsts, heads, heads_z, head_y, tails, x_hi, x_lo, y_hi, y_lo, part, swap_in, far_in, near_in, last_in,
    load_sem, own_sem, fan_send, fan_recv, fan_own, head_send, head_recv, ring_send, ring_recv, z_send, z_recv,
    core_send, core_recv, swap_send, swap_recv, far_send, far_recv, near_send, near_recv, last_send, last_recv, last_own, ready,
):
    tm, zl, c = lax.axis_index("tm"), lax.axis_index("row"), lax.axis_index("col")
    y, x, zh = lax.div(tm, 8), lax.rem(lax.div(tm, 2), 4), lax.rem(tm, 2)
    b = zl * 2 + c
    b_z, b_core, b_both = (1 - zl) * 2 + c, zl * 2 + 1 - c, (1 - zl) * 2 + 1 - c

    def at(yy, xx, zz, row, col):
        return (lax.rem(yy, 4) * 8 + lax.rem(xx, 4) * 2 + zz, row, col)

    def along_x(d):
        return at(y, x + d, zh, zl, c)

    def along_y(d):
        return at(y + d, x, zh, zl, c)

    other_z = (tm, 1 - zl, c)
    other_core = (tm, zl, 1 - c)
    other_half = at(y, x, 1 - zh, zl, c)

    barrier = pltpu.get_barrier_semaphore()
    peers = [along_x(1), along_x(3), along_x(2), along_y(1), along_y(3), other_z, other_core, other_half]
    for peer in peers:
        pl.semaphore_signal(barrier, inc=1, device_id=peer, device_id_type=MESH)

    def channels_of(q):
        return pl.ds(pl.multiple_of(lax.rem(x + q, 4) * LANES, LANES), LANES)

    loads = {}
    for q in (0, 1, 3, 2):
        loads[q] = pltpu.make_async_copy(s_ref.at[:, channels_of(q)], blocks.at[0, q], load_sem.at[q])
        loads[q].start()
    pl.semaphore_wait(barrier, len(peers))

    sent = []

    def send(src, dst, send_sem, recv_sem, device):
        copy = pltpu.make_async_remote_copy(
            src_ref=src, dst_ref=dst, send_sem=send_sem, recv_sem=recv_sem, device_id=device, device_id_type=MESH
        )
        copy.start()
        sent.append(copy)
        return copy

    whole = pl.ds(0, LEN)
    parts = (pl.ds(0, LEN // 2), pl.ds(LEN // 2, LEN // 2))

    def ring(n, way, d, q, rows=whole):
        return send(
            blocks.at[d, q, rows],
            blocks.at[(d - way) % 4, (q - way) % 4, rows],
            ring_send.at[n],
            ring_recv.at[n],
            along_x(way % 4),
        )

    fans = []
    for d in range(1, 4):
        fans.append(
            send(s_ref.at[pl.ds(0, LAGS), channels_of(d)], heads.at[x], fan_send.at[4 - d], fan_recv.at[4 - d], along_x(d))
        )
    fan_mine = pltpu.make_async_copy(s_ref.at[pl.ds(0, LAGS), channels_of(0)], heads.at[x], fan_own.at[0])
    fan_mine.start()

    left_0, right_0 = [], []
    for h in range(2):
        for n, way, q, to in ((h, 1, 1, left_0), (2 + h, -1, 3, right_0)):
            to.append(
                send(
                    s_ref.at[parts[h], channels_of(q)],
                    blocks.at[-way % 4, 0, parts[h]],
                    ring_send.at[n],
                    ring_recv.at[n],
                    along_x(way % 4),
                )
            )
    for q in range(4):
        loads[q].wait()

    z_copies, core_copies, own_copies = {}, {}, {}
    tail = pl.ds(LEN, LAGS)
    farthest = lax.rem(y + 2, 4)
    later = jnp.logical_or(b_core == farthest, b == y)
    later_z = jnp.logical_or(b_both == farthest, b_z == y)

    def cross(d, n, rows):
        z_copies[n] = pltpu.make_async_remote_copy(
            src_ref=blocks.at[d, 0, rows],
            dst_ref=firsts.at[b, d, rows],
            send_sem=z_send.at[n],
            recv_sem=z_recv.at[n],
            device_id=other_z,
            device_id_type=MESH,
        )
        sent.append(z_copies[n])
        if d in (1, 2):
            pl.when(jnp.logical_not(later))(z_copies[n].start)
        else:
            z_copies[n].start()
        core_copies[n] = send(
            blocks.at[d, 0, rows], firsts.at[b, d, rows], core_send.at[0, n], core_recv.at[0, n], other_core
        )
        own_copies[n] = pltpu.make_async_copy(blocks.at[d, 0, rows], firsts.at[b, d, rows], own_sem.at[n])
        own_copies[n].start()

    def pass_on(n):
        z_copies[n].wait_recv()
        core_copies[6 + n].start()

    def late(do, which=(2, 4)):
        for n in which:
            do(n)

    for n in range(6):
        d, rows = (2, parts[n // 4]) if n in (2, 4) else (n, whole)
        src = firsts.at[b_z, :, tail] if n == 5 else firsts.at[b_z, d, rows]
        core_copies[6 + n] = pltpu.make_async_remote_copy(
            src_ref=src,
            dst_ref=src,
            send_sem=core_send.at[1, n],
            recv_sem=core_recv.at[1, n],
            device_id=other_core,
            device_id_type=MESH,
        )
        sent.append(core_copies[6 + n])

    cross(0, 0, whole)
    fan_mine.wait()
    for copy in fans:
        copy.wait_recv()
    over_z = send(heads, heads_z, head_send.at[0], head_recv.at[0], other_half)

    def seconds(first, q, d):
        cols = slice(q * LANES, (q + 1) * LANES)
        for r in range(LAGS):
            hi, lo = halves(blocks[d, first + q, pl.ds(r, PER, stride=LAGS), :])
            to = pl.ds(pl.multiple_of(r * DEEP + d * PER, PER), PER)
            y_hi[to, cols] = hi
            y_lo[to, cols] = lo

    left_0[0].wait_recv()
    right_0[0].wait_recv()
    left_1, right_1, from_far, far_1 = [], [], [], []
    for h in range(2):
        left_1.append(ring(4 + h, 1, 0, 2, parts[h]))
        right_1.append(ring(6 + h, -1, 0, 0, parts[h]))
    left_0[1].wait_recv()
    cross(3, 3, whole)
    right_0[1].wait_recv()
    cross(1, 1, whole)
    over_z.wait_recv()
    over_y = send(heads_z.at[0], head_y, head_send.at[1], head_recv.at[1], along_y(3))
    seconds(0, 0, 0)
    seconds(0, 1, 0)
    for h in range(2):
        left_1[h].wait_recv()
        from_far.append(ring(8 + h, 1, 3, 1, parts[h]))
        far_1.append(ring(10 + h, -1, 1, 0, parts[h]))
    over_y.wait_recv()
    for d in range(4):
        place = lax.rem(x + d, 4)
        beyond = jnp.where(y == 3, jnp.zeros((LAGS, LANES), F32), head_y[...])
        after = jnp.where(place == 3, beyond, heads_z[lax.rem(place + 1, 4)])
        tails[d] = jnp.where(zh == 0, heads_z[place], after)
    z_copies[5] = send(tails, firsts.at[b, :, tail], z_send.at[5], z_recv.at[5], other_z)
    core_copies[5] = send(tails, firsts.at[b, :, tail], core_send.at[0, 5], core_recv.at[0, 5], other_core)
    own_copies[5] = pltpu.make_async_copy(tails, firsts.at[b, :, tail], own_sem.at[5])
    own_copies[5].start()
    pass_on(0)
    for h in range(2):
        right_1[h].wait_recv()
    seconds(0, 0, 3)
    seconds(0, 1, 3)
    seconds(0, 0, 1)
    seconds(0, 1, 1)
    for h in range(2):
        from_far[h].wait_recv()
        cross(2, 2 + 2 * h, parts[h])
    pl.when(later)(lambda: late(lambda n: z_copies[n].start(), (1,)))
    rest = [ring(12, 1, 0, 3), ring(13, -1, 0, 1), ring(14, -1, 1, 1), ring(15, 1, 0, 0), ring(16, -1, 0, 2), ring(17, 1, 3, 0)]
    for h in range(2):
        far_1[h].wait_recv()
    seconds(0, 0, 2)
    seconds(0, 1, 2)
    for n in (3, 5):
        pass_on(n)
    pl.when(jnp.logical_not(later_z))(lambda: pass_on(1))

    def arrived(bb):
        @pl.when(bb == b)
        def _():
            for n in range(6):
                own_copies[n].wait()

        @pl.when(bb == b_core)
        def _():
            for n in range(6):
                core_copies[n].wait_recv()

        @pl.when(bb == b_both)
        def _():
            for n in range(6):
                core_copies[6 + n].wait_recv()

    def spread(bb):
        for m in range(1, 2 * LAGS):
            v = jnp.concatenate([firsts[bb, d, pl.ds(m, PER, stride=LAGS), :] for d in range(4)], axis=0)
            hi, lo = halves(v.T)
            lanes = slice((m - 1) * DEEP, m * DEEP)
            x_hi[bb, :, lanes] = hi
            x_lo[bb, :, lanes] = lo

    ends = (1, 3)
    lanes = (pl.ds(0, LANES), pl.ds(LANES, LANES))
    mine = pl.ds(pl.multiple_of(zh * 64, 64), 64)
    yours = pl.ds(pl.multiple_of((1 - zh) * 64, 64), 64)

    def remote(src, dst, send_sem, recv_sem, device):
        return pltpu.make_async_remote_copy(
            src_ref=src, dst_ref=dst, send_sem=send_sem, recv_sem=recv_sem, device_id=device, device_id_type=MESH
        )

    def whole_sums(chunk, f, u):
        return f == 0 or (chunk, u) in STRAIGHT

    def swap(chunk, e, n):
        if e not in ends:
            src, dst = part.at[chunk, e, n, :, :, yours, lanes[1]], swap_in.at[chunk, e, n]
        elif whole_sums(chunk, 1, 1):
            src, dst = part.at[chunk, e, 0, n, :, yours, lanes[1]], swap_in.at[chunk, e, 0, n]
        else:
            src, dst = part.at[chunk, e, :, n, :, yours, lanes[1]], swap_in.at[chunk, e, :, n]
        return remote(src, dst, swap_send.at[chunk, e, n], swap_recv.at[chunk, e, n], other_half)

    def add_swap(chunk, e, n):
        swap(chunk, e, n).wait_recv()
        if e not in ends:
            part[chunk, e, n, :, :, mine, lanes[1]] += swap_in[chunk, e, n]
        elif whole_sums(chunk, 1, 1):
            part[chunk, e, 0, n, :, mine, lanes[1]] += swap_in[chunk, e, 0, n]
        else:
            part[chunk, e, :, n, :, mine, lanes[1]] += swap_in[chunk, e, :, n]

    def span(chunk, f, u):
        return (pl.ds(0, LANES), pl.ds(0, LANES)) if whole_sums(chunk, f, u) else (mine, pl.ds(0, 64))

    def far(chunk, f, way, u):
        here, there = span(chunk, f, u)
        return remote(
            part.at[chunk, 2, u, way, :, here, lanes[f]],
            far_in.at[chunk, f, way, u, :, there],
            far_send.at[chunk, f, way, u],
            far_recv.at[chunk, f, way, u],
            along_y(ends[way]),
        )

    def near(chunk, f, way, u, w):
        here, there = span(chunk, f, u)
        return remote(
            part.at[chunk, ends[way], u, w, :, here, lanes[f]],
            near_in.at[chunk, f, way, u, w, :, there],
            near_send.at[chunk, f, way, u, w],
            near_recv.at[chunk, f, way, u, w],
            along_y(ends[way]),
        )

    def kinds(chunk, straight):
        return [(f, u) for f in range(2) for u in range(2) if whole_sums(chunk, f, u) == straight]

    def add_far(chunk, straight):
        for f, u in kinds(chunk, straight):
            here, there = span(chunk, f, u)
            for way in range(2):
                far(chunk, f, way, u).wait_recv()
                part[chunk, ends[way], u, way, :, here, lanes[f]] += far_in[chunk, f, way, u, :, there]
                near(chunk, f, way, u, way).start()

    def after_product(chunk, j):
        if j < 2:
            for f, u in kinds(chunk, True):
                if u == j:
                    for way in range(2):
                        far(chunk, f, way, u).start()
            if not whole_sums(chunk, 1, j):
                swap(chunk, 2, j).start()
        elif j < 6:
            way = j % 2
            n = 1 - way if j < 4 else way
            if j < 4:
                for f, u in kinds(chunk, True):
                    near(chunk, f, way, u, 1 - way).start()
            swap(chunk, ends[way], n).start()
        elif not whole_sums(chunk, 1, j - 6):
            swap(chunk, 0, j - 6).start()

    def after_step(chunk, p):
        if p == 4:
            for f, u in kinds(chunk, False):
                add_swap(chunk, 2, u)
                for way in range(2):
                    far(chunk, f, way, u).start()
        if p == 5:
            add_far(chunk, True)
        if p == 6:
            for way in range(2):
                add_swap(chunk, ends[way], 1 - way)
                for f, u in kinds(chunk, False):
                    near(chunk, f, way, u, 1 - way).start()
        if p == 7:
            for way in range(2):
                add_swap(chunk, ends[way], way)
            add_far(chunk, False)

    def before(s):
        if s == 0:
            pl.when(later)(lambda: late(lambda n: z_copies[n].start()))
        if s == 2:
            pl.when(jnp.logical_not(later_z))(lambda: late(pass_on))
        if s == 4:
            pl.when(later_z)(lambda: late(pass_on, (1, 2, 4)))
        if s == 8:
            pl.semaphore_signal(ready, inc=1, device_id=other_half, device_id_type=MESH)
            for copy in rest:
                copy.wait_recv()

            def one(d, carry):
                for q in range(2):
                    seconds(2, q, d)
                return carry

            lax.fori_loop(0, 4, one, 0)

    far_here = zl == lax.div(farthest, 2)
    near_first = jnp.where(far_here, 1 - lax.rem(y, 2), lax.rem(y, 2))

    def step(s, carry):
        chunk, p = lax.div(s, 8), lax.rem(s, 8)
        by_far = jnp.logical_or(far_here, chunk == 1)
        second = lax.rem(p, 2)
        near_l = jnp.where(p < 4, 2, 4) + jnp.where(second == 0, near_first, 1 - near_first)
        near_r = jnp.where(p < 2, near_first, 1 - near_first) + 2 * second + 2
        order_l = jnp.where(jnp.logical_and(p >= 2, p < 6), near_l, p)
        order_r = jnp.where(p >= 6, p, jnp.where(jnp.logical_and(p >= 2, p < 4), p - 2, near_r))
        j = jnp.where(by_far, order_l, order_r)
        odd = lax.rem(j, 2)
        e = jnp.where(j < 2, 2, jnp.where(j < 6, 1 + 2 * odd, 0))
        bb = lax.rem(y + e, 4)
        for i in (0, 2, 4, 8):
            pl.when(s == i)(lambda i=i: before(i))
        fresh = jnp.logical_or(jnp.logical_or(s == 0, s == 2), jnp.logical_or(s == 6, s == jnp.where(far_here, 3, 4)))

        @pl.when(fresh)
        def _():
            arrived(bb)
            spread(bb)

        by_way = jnp.logical_and(j >= 2, j < 6)
        w = jnp.where(j < 4, 1 - odd, odd)
        pairs = [
            (jnp.where(by_way, 0, odd), jnp.where(by_way, w, 0)),
            (jnp.where(by_way, 1, odd), jnp.where(by_way, w, 1)),
        ]
        for u, w in pairs:
            pass

        def dots(n, carry):
            starts = [
                pl.multiple_of( (u * 4 + w * 2 + i) * DEEP, LANES) for u, w in pairs for i in range(2)
            ]
            lhs_hi = jnp.concatenate([x_hi[bb, :, pl.ds(start, LAGS * DEEP)] for start in starts], axis=0)
            lhs_lo = jnp.concatenate([x_lo[bb, :, pl.ds(start, LAGS * DEEP)] for start in starts], axis=0)
            deep = pl.ds(0, LAGS * DEEP)
            rhs_hi, rhs_lo = y_hi[deep, :], y_lo[deep, :]
            got = jnp.dot(lhs_hi, rhs_hi, preferred_element_type=F32)
            got += jnp.dot(lhs_lo, rhs_hi, preferred_element_type=F32)
            got += jnp.dot(lhs_hi, rhs_lo, preferred_element_type=F32)
            got = got.reshape(2, 2, LANES, WIDE)
            for n, (u, w) in enumerate(pairs):
                part[chunk, e, u, w] = got[n]
            return carry

        dots(0, 0)
        for i in range(16):
            pl.when(jnp.logical_and(chunk == i // 8, j == i % 8))(lambda i=i: after_product(i // 8, i % 8))
        for i in (4, 5, 6, 7, 12, 13, 14, 15):
            pl.when(s == i)(lambda i=i: after_step(i // 8, i % 8))

        @pl.when(s == 10)
        def _():
            pl.semaphore_wait(ready, 1)
            finish(0, 0)
            finish(0, 1)

        return carry

    def total(chunk, f, u):
        here, there = span(chunk, f, u)
        for way in range(2):
            for w in range(2):
                near(chunk, f, way, u, w).wait_recv()
        part[chunk, 0, u, :, :, here, lanes[f]] += (
            near_in[chunk, f, 0, u, :, :, there] + near_in[chunk, f, 1, u, :, :, there]
        )

    def deals(chunk, f, u):
        straight = whole_sums(chunk, f, u)
        half = zh if straight else 0
        for other in range(2 if straight else 1):
            for row in range(2):
                zz = lax.rem(zh + other, 2)
                src = part.at[chunk, 0, u, :, :, pl.ds(pl.multiple_of((zz * 2 + row) * 32, 32), 32), lanes[f]]
                dst = last_in.at[chunk, f, u, c, half]
                copy = remote(
                    src,
                    dst,
                    last_send.at[chunk, f, u, other, row],
                    last_recv.at[chunk, f, u, c, half],
                    at(y, x, zz, row, zl),
                )
                if other == 0:
                    here = jnp.logical_and(row == zl, zl == c)
                    yield here, copy, pltpu.make_async_copy(src, dst, last_own.at[chunk, f, u])
                else:
                    yield None, copy, None

    def finish(chunk, f, units=(0, 1)):
        for u in units:
            if not whole_sums(chunk, f, u):
                add_swap(chunk, 0, u)
            total(chunk, f, u)
            for here, copy, own in deals(chunk, f, u):
                if here is None:
                    copy.start()
                else:
                    pl.when(jnp.logical_not(here))(copy.start)
                    pl.when(here)(own.start)

    scale = [np.float32(1.0 / np.sqrt(np.float32(SAMPLES - k))) for k in range(1, LAGS + 1)]

    def write(chunk, f, units=(0, 1)):
        channels = lax.rem(x + 2 * chunk + f, 4)
        for u in units:
            for here, copy, own in deals(chunk, f, u):
                if here is None:
                    copy.wait_send()
                else:
                    pl.when(jnp.logical_not(here))(copy.wait_send)
                    pl.when(here)(own.wait)
            straight = whole_sums(chunk, f, u)
            for cc in range(2):
                for hh in range(2 if straight else 1):
                    same = jnp.logical_and(zl == c, cc == c)
                    if straight:
                        same = jnp.logical_and(same, hh == zh)
                    place = last_in.at[chunk, f, u, cc, hh]
                    copy = remote(
                        place, place, last_send.at[chunk, f, u, 0, 0], last_recv.at[chunk, f, u, cc, hh], other_z
                    )
                    pl.when(jnp.logical_not(same))(copy.wait_recv)
            for cc in range(2):
                to = pl.ds(pl.multiple_of(cc * 4 * LANES + channels * LANES, LANES), LANES)
                for w in range(2):
                    for i in range(2):
                        k = u * 4 + w * 2 + i
                        got = last_in[chunk, f, u, cc, 0, w, i]
                        if straight:
                            got += last_in[chunk, f, u, cc, 1, w, i]
                        out_ref[:, k, to] = got * scale[k]

    lax.fori_loop(0, 16, step, 0)
    write(0, 0)
    write(0, 1)
    finish(1, 0)
    finish(1, 1, (1, 0))
    write(1, 0)
    write(1, 1, (1, 0))
    for copy in sent:
        copy.wait_send()

    for chunk in range(2):
        for n in range(2):
            for e in range(4):
                if e in ends or not whole_sums(chunk, 1, n):
                    swap(chunk, e, n).wait_send()
        for f in range(2):
            for way in range(2):
                for u in range(2):
                    far(chunk, f, way, u).wait_send()
                    for w in range(2):
                        near(chunk, f, way, u, w).wait_send()


def shards(strain):
    dma, vmem = pltpu.SemaphoreType.DMA, pltpu.VMEM
    return pl.pallas_call(
        kernel,
        out_shape=jax.ShapeDtypeStruct((32, LAGS, 8 * LANES), F32),
        in_specs=[pl.BlockSpec(memory_space=pl.ANY)],
        out_specs=pl.BlockSpec(memory_space=pltpu.VMEM),
        scratch_shapes=[
            vmem((4, 4, LEN, LANES), F32),
            vmem((4, 4, LEN + LAGS, LANES), F32),
            vmem((4, LAGS, LANES), F32),
            vmem((4, LAGS, LANES), F32),
            vmem((LAGS, LANES), F32),
            vmem((4, LAGS, LANES), F32),
            vmem((4, LANES, (2 * LAGS - 1) * DEEP), BF16),
            vmem((4, LANES, (2 * LAGS - 1) * DEEP), BF16),
            vmem((LAGS * DEEP, WIDE), BF16),
            vmem((LAGS * DEEP, WIDE), BF16),
            vmem((2, 4, 2, 2, 2, LANES, WIDE), F32),
            vmem((2, 4, 2, 2, 2, 64, LANES), F32),
            vmem((2, 2, 2, 2, 2, LANES, LANES), F32),
            vmem((2, 2, 2, 2, 2, 2, LANES, LANES), F32),
            vmem((2, 2, 2, 2, 2, 2, 2, 32, LANES), F32),
            dma((4,)), dma((6,)), dma((4,)), dma((4,)), dma((1,)), dma((2,)), dma((2,)), dma((18,)), dma((18,)),
            dma((6,)), dma((6,)), dma((2, 6)), dma((2, 6)), dma((2, 4, 2)), dma((2, 4, 2)),
            dma((2, 2, 2, 2)), dma((2, 2, 2, 2)), dma((2, 2, 2, 2, 2)), dma((2, 2, 2, 2, 2)),
            dma((2, 2, 2, 2, 2)), dma((2, 2, 2, 2, 2)), dma((2, 2, 2)),
            pltpu.SemaphoreType.REGULAR,
        ],
        compiler_params=pltpu.CompilerParams(
            collective_id=0, has_side_effects=True, vmem_limit_bytes=60 * 2**20
        ),
        cost_estimate=pl.CostEstimate(flops=3 * 2 * 8 * 512 * 512 * 3072, bytes_accessed=2**22, transcendentals=0),
    )(strain)


def solution(mesh):
    placed = (P("tm", ("row", "col")),)
    return jax.shard_map(
        shards, mesh=mesh, in_specs=placed, out_specs=P(("tm", "row"), None, "col"), check_vma=False
    )
```

```python
import jax
import jax.numpy as jnp
import numpy as np
from jax import lax
from jax.experimental import pallas as pl
from jax.experimental.pallas import tpu as pltpu
from jax.sharding import PartitionSpec as P

MESH = pl.DeviceIdType.MESH
LAGS = 8
SAMPLES = 24576
LEN = 768
LANES = 128
PER = LEN // LAGS
DEEP = 4 * PER
WIDE = 2 * LANES
STRAIGHT = ((1, 1),)
F32 = jnp.float32
BF16 = jnp.bfloat16


def halves(v):
    hi = v.astype(BF16)
    return hi, (v - hi.astype(F32)).astype(BF16)


def kernel(
    s_ref, out_ref, blocks, firsts, heads, heads_z, head_y, tails, x_hi, x_lo, y_hi, y_lo, part, swap_in, far_in, near_in, last_in,
    load_sem, own_sem, fan_send, fan_recv, fan_own, head_send, head_recv, ring_send, ring_recv, z_send, z_recv,
    core_send, core_recv, swap_send, swap_recv, far_send, far_recv, near_send, near_recv, last_send, last_recv, last_own, ready,
):
    tm, zl, c = lax.axis_index("tm"), lax.axis_index("row"), lax.axis_index("col")
    y, x, zh = lax.div(tm, 8), lax.rem(lax.div(tm, 2), 4), lax.rem(tm, 2)
    b = zl * 2 + c
    b_z, b_core, b_both = (1 - zl) * 2 + c, zl * 2 + 1 - c, (1 - zl) * 2 + 1 - c

    def at(yy, xx, zz, row, col):
        return (lax.rem(yy, 4) * 8 + lax.rem(xx, 4) * 2 + zz, row, col)

    def along_x(d):
        return at(y, x + d, zh, zl, c)

    def along_y(d):
        return at(y + d, x, zh, zl, c)

    other_z = (tm, 1 - zl, c)
    other_core = (tm, zl, 1 - c)
    other_half = at(y, x, 1 - zh, zl, c)

    barrier = pltpu.get_barrier_semaphore()
    peers = [along_x(1), along_x(3), along_x(2), along_y(1), along_y(3), other_z, other_core, other_half]
    for peer in peers:
        pl.semaphore_signal(barrier, inc=1, device_id=peer, device_id_type=MESH)

    def channels_of(q):
        return pl.ds(pl.multiple_of(lax.rem(x + q, 4) * LANES, LANES), LANES)

    loads = {}
    for q in (0, 1, 3, 2):
        loads[q] = pltpu.make_async_copy(s_ref.at[:, channels_of(q)], blocks.at[0, q], load_sem.at[q])
        loads[q].start()
    pl.semaphore_wait(barrier, len(peers))

    sent = []

    def send(src, dst, send_sem, recv_sem, device):
        copy = pltpu.make_async_remote_copy(
            src_ref=src, dst_ref=dst, send_sem=send_sem, recv_sem=recv_sem, device_id=device, device_id_type=MESH
        )
        copy.start()
        sent.append(copy)
        return copy

    whole = pl.ds(0, LEN)
    parts = (pl.ds(0, LEN // 2), pl.ds(LEN // 2, LEN // 2))

    def ring(n, way, d, q, rows=whole):
        return send(
            blocks.at[d, q, rows],
            blocks.at[(d - way) % 4, (q - way) % 4, rows],
            ring_send.at[n],
            ring_recv.at[n],
            along_x(way % 4),
        )

    fans = []
    for d in range(1, 4):
        fans.append(
            send(s_ref.at[pl.ds(0, LAGS), channels_of(d)], heads.at[x], fan_send.at[4 - d], fan_recv.at[4 - d], along_x(d))
        )
    fan_mine = pltpu.make_async_copy(s_ref.at[pl.ds(0, LAGS), channels_of(0)], heads.at[x], fan_own.at[0])
    fan_mine.start()

    left_0, right_0 = [], []
    for h in range(2):
        for n, way, q, to in ((h, 1, 1, left_0), (2 + h, -1, 3, right_0)):
            to.append(
                send(
                    s_ref.at[parts[h], channels_of(q)],
                    blocks.at[-way % 4, 0, parts[h]],
                    ring_send.at[n],
                    ring_recv.at[n],
                    along_x(way % 4),
                )
            )
    for q in range(4):
        loads[q].wait()

    z_copies, core_copies, own_copies = {}, {}, {}
    tail = pl.ds(LEN, LAGS)
    farthest = lax.rem(y + 2, 4)
    later = jnp.logical_or(b_core == farthest, b == y)
    later_z = jnp.logical_or(b_both == farthest, b_z == y)

    def cross(d, n, rows):
        z_copies[n] = pltpu.make_async_remote_copy(
            src_ref=blocks.at[d, 0, rows],
            dst_ref=firsts.at[b, d, rows],
            send_sem=z_send.at[n],
            recv_sem=z_recv.at[n],
            device_id=other_z,
            device_id_type=MESH,
        )
        sent.append(z_copies[n])
        if d in (1, 2):
            pl.when(jnp.logical_not(later))(z_copies[n].start)
        else:
            z_copies[n].start()
        core_copies[n] = send(
            blocks.at[d, 0, rows], firsts.at[b, d, rows], core_send.at[0, n], core_recv.at[0, n], other_core
        )
        own_copies[n] = pltpu.make_async_copy(blocks.at[d, 0, rows], firsts.at[b, d, rows], own_sem.at[n])
        own_copies[n].start()

    def pass_on(n):
        z_copies[n].wait_recv()
        core_copies[6 + n].start()

    def late(do, which=(2, 4)):
        for n in which:
            do(n)

    for n in range(6):
        d, rows = (2, parts[n // 4]) if n in (2, 4) else (n, whole)
        src = firsts.at[b_z, :, tail] if n == 5 else firsts.at[b_z, d, rows]
        core_copies[6 + n] = pltpu.make_async_remote_copy(
            src_ref=src,
            dst_ref=src,
            send_sem=core_send.at[1, n],
            recv_sem=core_recv.at[1, n],
            device_id=other_core,
            device_id_type=MESH,
        )
        sent.append(core_copies[6 + n])

    cross(0, 0, whole)
    fan_mine.wait()
    for copy in fans:
        copy.wait_recv()
    over_z = send(heads, heads_z, head_send.at[0], head_recv.at[0], other_half)

    def seconds(first, q, d):
        cols = slice(q * LANES, (q + 1) * LANES)
        for r in range(LAGS):
            hi, lo = halves(blocks[d, first + q, pl.ds(r, PER, stride=LAGS), :])
            to = pl.ds(pl.multiple_of(r * DEEP + d * PER, PER), PER)
            y_hi[to, cols] = hi
            y_lo[to, cols] = lo

    left_0[0].wait_recv()
    right_0[0].wait_recv()
    left_1, right_1, from_far, far_1 = [], [], [], []
    for h in range(2):
        left_1.append(ring(4 + h, 1, 0, 2, parts[h]))
        right_1.append(ring(6 + h, -1, 0, 0, parts[h]))
    left_0[1].wait_recv()
    cross(3, 3, whole)
    right_0[1].wait_recv()
    cross(1, 1, whole)
    over_z.wait_recv()
    over_y = send(heads_z.at[0], head_y, head_send.at[1], head_recv.at[1], along_y(3))
    seconds(0, 0, 0)
    seconds(0, 1, 0)
    for h in range(2):
        left_1[h].wait_recv()
        from_far.append(ring(8 + h, 1, 3, 1, parts[h]))
        far_1.append(ring(10 + h, -1, 1, 0, parts[h]))
    over_y.wait_recv()
    for d in range(4):
        place = lax.rem(x + d, 4)
        beyond = jnp.where(y == 3, jnp.zeros((LAGS, LANES), F32), head_y[...])
        after = jnp.where(place == 3, beyond, heads_z[lax.rem(place + 1, 4)])
        tails[d] = jnp.where(zh == 0, heads_z[place], after)
    z_copies[5] = send(tails, firsts.at[b, :, tail], z_send.at[5], z_recv.at[5], other_z)
    core_copies[5] = send(tails, firsts.at[b, :, tail], core_send.at[0, 5], core_recv.at[0, 5], other_core)
    own_copies[5] = pltpu.make_async_copy(tails, firsts.at[b, :, tail], own_sem.at[5])
    own_copies[5].start()
    pass_on(0)
    for h in range(2):
        right_1[h].wait_recv()
    seconds(0, 0, 3)
    seconds(0, 1, 3)
    seconds(0, 0, 1)
    seconds(0, 1, 1)
    for h in range(2):
        from_far[h].wait_recv()
        cross(2, 2 + 2 * h, parts[h])
    pl.when(later)(lambda: late(lambda n: z_copies[n].start(), (1,)))
    rest = [ring(12, 1, 0, 3), ring(13, -1, 0, 1), ring(14, -1, 1, 1), ring(15, 1, 0, 0), ring(16, -1, 0, 2), ring(17, 1, 3, 0)]
    for h in range(2):
        far_1[h].wait_recv()
    seconds(0, 0, 2)
    seconds(0, 1, 2)
    for n in (3, 5):
        pass_on(n)
    pl.when(jnp.logical_not(later_z))(lambda: pass_on(1))

    def arrived(bb):
        @pl.when(bb == b)
        def _():
            for n in range(6):
                own_copies[n].wait()

        @pl.when(bb == b_core)
        def _():
            for n in range(6):
                core_copies[n].wait_recv()

        @pl.when(bb == b_both)
        def _():
            for n in range(6):
                core_copies[6 + n].wait_recv()

    def spread(bb):
        for m in range(1, 2 * LAGS):
            v = jnp.concatenate([firsts[bb, d, pl.ds(m, PER, stride=LAGS), :] for d in range(4)], axis=0)
            hi, lo = halves(v.T)
            lanes = slice((m - 1) * DEEP, m * DEEP)
            x_hi[bb, :, lanes] = hi
            x_lo[bb, :, lanes] = lo

    ends = (1, 3)
    lanes = (pl.ds(0, LANES), pl.ds(LANES, LANES))
    mine = pl.ds(pl.multiple_of(zh * 64, 64), 64)
    yours = pl.ds(pl.multiple_of((1 - zh) * 64, 64), 64)

    def remote(src, dst, send_sem, recv_sem, device):
        return pltpu.make_async_remote_copy(
            src_ref=src, dst_ref=dst, send_sem=send_sem, recv_sem=recv_sem, device_id=device, device_id_type=MESH
        )

    def whole_sums(chunk, f, u):
        return f == 0 or (chunk, u) in STRAIGHT

    def swap(chunk, e, n):
        if e not in ends:
            src, dst = part.at[chunk, e, n, :, :, yours, lanes[1]], swap_in.at[chunk, e, n]
        elif whole_sums(chunk, 1, 1):
            src, dst = part.at[chunk, e, 0, n, :, yours, lanes[1]], swap_in.at[chunk, e, 0, n]
        else:
            src, dst = part.at[chunk, e, :, n, :, yours, lanes[1]], swap_in.at[chunk, e, :, n]
        return remote(src, dst, swap_send.at[chunk, e, n], swap_recv.at[chunk, e, n], other_half)

    def add_swap(chunk, e, n):
        swap(chunk, e, n).wait_recv()
        if e not in ends:
            part[chunk, e, n, :, :, mine, lanes[1]] += swap_in[chunk, e, n]
        elif whole_sums(chunk, 1, 1):
            part[chunk, e, 0, n, :, mine, lanes[1]] += swap_in[chunk, e, 0, n]
        else:
            part[chunk, e, :, n, :, mine, lanes[1]] += swap_in[chunk, e, :, n]

    def span(chunk, f, u):
        return (pl.ds(0, LANES), pl.ds(0, LANES)) if whole_sums(chunk, f, u) else (mine, pl.ds(0, 64))

    def far(chunk, f, way, u):
        here, there = span(chunk, f, u)
        return remote(
            part.at[chunk, 2, u, way, :, here, lanes[f]],
            far_in.at[chunk, f, way, u, :, there],
            far_send.at[chunk, f, way, u],
            far_recv.at[chunk, f, way, u],
            along_y(ends[way]),
        )

    def near(chunk, f, way, u, w):
        here, there = span(chunk, f, u)
        return remote(
            part.at[chunk, ends[way], u, w, :, here, lanes[f]],
            near_in.at[chunk, f, way, u, w, :, there],
            near_send.at[chunk, f, way, u, w],
            near_recv.at[chunk, f, way, u, w],
            along_y(ends[way]),
        )

    def kinds(chunk, straight):
        return [(f, u) for f in range(2) for u in range(2) if whole_sums(chunk, f, u) == straight]

    def add_far(chunk, straight):
        for f, u in kinds(chunk, straight):
            here, there = span(chunk, f, u)
            for way in range(2):
                far(chunk, f, way, u).wait_recv()
                part[chunk, ends[way], u, way, :, here, lanes[f]] += far_in[chunk, f, way, u, :, there]
                near(chunk, f, way, u, way).start()

    def after_product(chunk, j):
        if j < 2:
            for f, u in kinds(chunk, True):
                if u == j:
                    for way in range(2):
                        far(chunk, f, way, u).start()
            if not whole_sums(chunk, 1, j):
                swap(chunk, 2, j).start()
        elif j < 6:
            way = j % 2
            n = 1 - way if j < 4 else way
            if j < 4:
                for f, u in kinds(chunk, True):
                    near(chunk, f, way, u, 1 - way).start()
            swap(chunk, ends[way], n).start()
        elif not whole_sums(chunk, 1, j - 6):
            swap(chunk, 0, j - 6).start()

    def after_step(chunk, p):
        if p == 4:
            for f, u in kinds(chunk, False):
                add_swap(chunk, 2, u)
                for way in range(2):
                    far(chunk, f, way, u).start()
        if p == 5:
            add_far(chunk, True)
        if p == 6:
            for way in range(2):
                add_swap(chunk, ends[way], 1 - way)
                for f, u in kinds(chunk, False):
                    near(chunk, f, way, u, 1 - way).start()
        if p == 7:
            for way in range(2):
                add_swap(chunk, ends[way], way)
            add_far(chunk, False)

    def before(s):
        if s == 0:
            pl.when(later)(lambda: late(lambda n: z_copies[n].start()))
        if s == 2:
            pl.when(jnp.logical_not(later_z))(lambda: late(pass_on))
        if s == 4:
            pl.when(later_z)(lambda: late(pass_on, (1, 2, 4)))
        if s == 8:
            pl.semaphore_signal(ready, inc=1, device_id=other_half, device_id_type=MESH)
            for copy in rest:
                copy.wait_recv()

            def one(d, carry):
                for q in range(2):
                    seconds(2, q, d)
                return carry

            lax.fori_loop(0, 4, one, 0)

    far_here = zl == lax.div(farthest, 2)
    near_first = jnp.where(far_here, 1 - lax.rem(y, 2), lax.rem(y, 2))

    def step(s, carry):
        chunk, p = lax.div(s, 8), lax.rem(s, 8)
        by_far = jnp.logical_or(far_here, chunk == 1)
        second = lax.rem(p, 2)
        near_l = jnp.where(p < 4, 2, 4) + jnp.where(second == 0, near_first, 1 - near_first)
        near_r = jnp.where(p < 2, near_first, 1 - near_first) + 2 * second + 2
        order_l = jnp.where(jnp.logical_and(p >= 2, p < 6), near_l, p)
        order_r = jnp.where(p >= 6, p, jnp.where(jnp.logical_and(p >= 2, p < 4), p - 2, near_r))
        j = jnp.where(by_far, order_l, order_r)
        odd = lax.rem(j, 2)
        e = jnp.where(j < 2, 2, jnp.where(j < 6, 1 + 2 * odd, 0))
        bb = lax.rem(y + e, 4)
        for i in (0, 2, 4, 8):
            pl.when(s == i)(lambda i=i: before(i))
        fresh = jnp.logical_or(jnp.logical_or(s == 0, s == 2), jnp.logical_or(s == 6, s == jnp.where(far_here, 3, 4)))

        @pl.when(fresh)
        def _():
            arrived(bb)
            spread(bb)

        by_way = jnp.logical_and(j >= 2, j < 6)
        w = jnp.where(j < 4, 1 - odd, odd)
        pairs = [
            (jnp.where(by_way, 0, odd), jnp.where(by_way, w, 0)),
            (jnp.where(by_way, 1, odd), jnp.where(by_way, w, 1)),
        ]
        for u, w in pairs:
            pass

        def dots(n, carry):
            starts = [
                pl.multiple_of( (u * 4 + w * 2 + i) * DEEP, LANES) for u, w in pairs for i in range(2)
            ]
            lhs_hi = jnp.concatenate([x_hi[bb, :, pl.ds(start, LAGS * DEEP)] for start in starts], axis=0)
            lhs_lo = jnp.concatenate([x_lo[bb, :, pl.ds(start, LAGS * DEEP)] for start in starts], axis=0)
            deep = pl.ds(0, LAGS * DEEP)
            rhs_hi, rhs_lo = y_hi[deep, :], y_lo[deep, :]
            got = jnp.dot(lhs_hi, rhs_hi, preferred_element_type=F32)
            got += jnp.dot(lhs_lo, rhs_hi, preferred_element_type=F32)
            got += jnp.dot(lhs_hi, rhs_lo, preferred_element_type=F32)
            got = got.reshape(2, 2, LANES, WIDE)
            for n, (u, w) in enumerate(pairs):
                part[chunk, e, u, w] = got[n]
            return carry

        dots(0, 0)
        for i in range(16):
            pl.when(jnp.logical_and(chunk == i // 8, j == i % 8))(lambda i=i: after_product(i // 8, i % 8))
        for i in (4, 5, 6, 7, 12, 13, 14, 15):
            pl.when(s == i)(lambda i=i: after_step(i // 8, i % 8))

        @pl.when(s == 10)
        def _():
            pl.semaphore_wait(ready, 1)
            finish(0, 0)
            finish(0, 1)

        return carry

    def total(chunk, f, u):
        here, there = span(chunk, f, u)
        for way in range(2):
            for w in range(2):
                near(chunk, f, way, u, w).wait_recv()
        part[chunk, 0, u, :, :, here, lanes[f]] += (
            near_in[chunk, f, 0, u, :, :, there] + near_in[chunk, f, 1, u, :, :, there]
        )

    def deals(chunk, f, u):
        straight = whole_sums(chunk, f, u)
        half = zh if straight else 0
        for other in range(2 if straight else 1):
            for row in range(2):
                zz = lax.rem(zh + other, 2)
                src = part.at[chunk, 0, u, :, :, pl.ds(pl.multiple_of((zz * 2 + row) * 32, 32), 32), lanes[f]]
                dst = last_in.at[chunk, f, u, c, half]
                copy = remote(
                    src,
                    dst,
                    last_send.at[chunk, f, u, other, row],
                    last_recv.at[chunk, f, u, c, half],
                    at(y, x, zz, row, zl),
                )
                if other == 0:
                    here = jnp.logical_and(row == zl, zl == c)
                    yield here, copy, pltpu.make_async_copy(src, dst, last_own.at[chunk, f, u])
                else:
                    yield None, copy, None

    def finish(chunk, f, units=(0, 1)):
        for u in units:
            if not whole_sums(chunk, f, u):
                add_swap(chunk, 0, u)
            total(chunk, f, u)
            for here, copy, own in deals(chunk, f, u):
                if here is None:
                    copy.start()
                else:
                    pl.when(jnp.logical_not(here))(copy.start)
                    pl.when(here)(own.start)

    scale = [np.float32(1.0 / np.sqrt(np.float32(SAMPLES - k))) for k in range(1, LAGS + 1)]

    def write(chunk, f, units=(0, 1)):
        channels = lax.rem(x + 2 * chunk + f, 4)
        for u in units:
            for here, copy, own in deals(chunk, f, u):
                if here is None:
                    copy.wait_send()
                else:
                    pl.when(jnp.logical_not(here))(copy.wait_send)
                    pl.when(here)(own.wait)
            straight = whole_sums(chunk, f, u)
            for cc in range(2):
                for hh in range(2 if straight else 1):
                    same = jnp.logical_and(zl == c, cc == c)
                    if straight:
                        same = jnp.logical_and(same, hh == zh)
                    place = last_in.at[chunk, f, u, cc, hh]
                    copy = remote(
                        place, place, last_send.at[chunk, f, u, 0, 0], last_recv.at[chunk, f, u, cc, hh], other_z
                    )
                    pl.when(jnp.logical_not(same))(copy.wait_recv)
            for cc in range(2):
                to = pl.ds(pl.multiple_of(cc * 4 * LANES + channels * LANES, LANES), LANES)
                for w in range(2):
                    for i in range(2):
                        k = u * 4 + w * 2 + i
                        got = last_in[chunk, f, u, cc, 0, w, i]
                        if straight:
                            got += last_in[chunk, f, u, cc, 1, w, i]
                        out_ref[:, k, to] = got * scale[k]

    def drain(chunk):
        for n in range(2):
            for e in range(4):
                if e in ends or not whole_sums(chunk, 1, n):
                    swap(chunk, e, n).wait_send()
        for f in range(2):
            for way in range(2):
                for u in range(2):
                    far(chunk, f, way, u).wait_send()
                    for w in range(2):
                        near(chunk, f, way, u, w).wait_send()

    lax.fori_loop(0, 16, step, 0)
    write(0, 0)
    write(0, 1)
    for copy in sent:
        copy.wait_send()
    drain(0)
    finish(1, 0)
    finish(1, 1, (1, 0))
    drain(1)
    write(1, 0)
    write(1, 1, (1, 0))


def shards(strain):
    dma, vmem = pltpu.SemaphoreType.DMA, pltpu.VMEM
    return pl.pallas_call(
        kernel,
        out_shape=jax.ShapeDtypeStruct((32, LAGS, 8 * LANES), F32),
        in_specs=[pl.BlockSpec(memory_space=pl.ANY)],
        out_specs=pl.BlockSpec(memory_space=pltpu.VMEM),
        scratch_shapes=[
            vmem((4, 4, LEN, LANES), F32),
            vmem((4, 4, LEN + LAGS, LANES), F32),
            vmem((4, LAGS, LANES), F32),
            vmem((4, LAGS, LANES), F32),
            vmem((LAGS, LANES), F32),
            vmem((4, LAGS, LANES), F32),
            vmem((4, LANES, (2 * LAGS - 1) * DEEP), BF16),
            vmem((4, LANES, (2 * LAGS - 1) * DEEP), BF16),
            vmem((LAGS * DEEP, WIDE), BF16),
            vmem((LAGS * DEEP, WIDE), BF16),
            vmem((2, 4, 2, 2, 2, LANES, WIDE), F32),
            vmem((2, 4, 2, 2, 2, 64, LANES), F32),
            vmem((2, 2, 2, 2, 2, LANES, LANES), F32),
            vmem((2, 2, 2, 2, 2, 2, LANES, LANES), F32),
            vmem((2, 2, 2, 2, 2, 2, 2, 32, LANES), F32),
            dma((4,)), dma((6,)), dma((4,)), dma((4,)), dma((1,)), dma((2,)), dma((2,)), dma((18,)), dma((18,)),
            dma((6,)), dma((6,)), dma((2, 6)), dma((2, 6)), dma((2, 4, 2)), dma((2, 4, 2)),
            dma((2, 2, 2, 2)), dma((2, 2, 2, 2)), dma((2, 2, 2, 2, 2)), dma((2, 2, 2, 2, 2)),
            dma((2, 2, 2, 2, 2)), dma((2, 2, 2, 2, 2)), dma((2, 2, 2)),
            pltpu.SemaphoreType.REGULAR,
        ],
        compiler_params=pltpu.CompilerParams(
            collective_id=0, has_side_effects=True, vmem_limit_bytes=60 * 2**20
        ),
        cost_estimate=pl.CostEstimate(flops=3 * 2 * 8 * 512 * 512 * 3072, bytes_accessed=2**22, transcendentals=0),
    )(strain)


def solution(mesh):
    placed = (P("tm", ("row", "col")),)
    return jax.shard_map(
        shards, mesh=mesh, in_specs=placed, out_specs=P(("tm", "row"), None, "col"), check_vma=False
    )
```
